256 devices in a mesh: prow: 32 (over x, z_hi, core), pcol: 8 (over z_lo, y).
Axes of the slice: x: 4, y: 4, z: 8 (z_hi: 4, z_lo: 2; z = z_hi * 2 + z_lo), core: 2. Of those that a mesh axis runs over, the one named last changes fastest.
Arguments:
- inverse_root: bfloat16 [16384, 16384], P('prow', 'pcol'), may hold values from -6 to 6
- panel: bfloat16 [16384, 8, 256], P('pcol', None, 'prow'), may hold values from -0.0625 to 0.0625
- block_mask: int32 [8, 64], replicated, may hold values 0 or 1
- diag_inverse: float32 [8, 256, 256], P(None, 'prow', 'pcol'), may hold values from -6 to 6
Outputs:
- panel_inverse: float32 [16384, 8, 256], P(('prow', 'pcol'))
- block_inverse: float32 [8, 256, 256], P(None, 'prow', 'pcol')
The draws below stay inside these ranges and needn't reach their ends.
All inputs are finite; a program needn't handle non-finite values.
Results may differ from the reference program's by a relative error of at most 0.0003.
Values may be sent and summed in bfloat16 or wider, within the bound.
No kernel may reach another device: no remote copies, remote signals or barrier semaphores. Data moves between devices by JAX's collectives and lax.ppermute only.
A program may use at most 64 MiB of HBM per device.

```python
import jax
import jax.numpy as jnp
from jax import lax

R = 16384
W = 256
NS = 8
RB = 64


def with_ends(entries, stream_key, low, high):
    spot = [jax.random.randint(jax.random.fold_in(stream_key, axis), (), 0, length) for axis, length in enumerate(entries.shape)]
    main_axis = entries.shape.index(max(entries.shape))
    neighbour = spot[:main_axis] + [(spot[main_axis] + 1) % entries.shape[main_axis]] + spot[main_axis + 1:]
    return entries.at[tuple(spot)].set(low).at[tuple(neighbour)].set(high)


def levels(rng, shape, pieces, least, high):
    factor_of, own = 1.0, jax.random.fold_in(rng, 6)
    for axis_at, shards_of in pieces:
        steps = jnp.exp(jax.random.uniform(jax.random.fold_in(own, axis_at), (shards_of,), jnp.float32, least / len(pieces), high / len(pieces)))
        factor_of = factor_of * jnp.repeat(steps, shape[axis_at] // shards_of).reshape([-1 if axis == axis_at else 1 for axis in range(len(shape))])
    return factor_of


def normal_values(stream_key, dims, width, limit, shards=(), dtype=jnp.bfloat16):
    drawn = jax.random.normal(stream_key, dims, jnp.float32) * width
    if len(shards) > 0:
        drawn = levels(stream_key, dims, shards, -0.22, 0.18) * drawn
    return jnp.clip(drawn, min=-limit, max=limit).astype(dtype)


def setup_inputs(seed: int = 0) -> dict:
    seeds = jax.random.split(jax.random.key(seed), 5)
    return {
        "inverse_root": normal_values(seeds[0], (R, R), 1.0, 6.0, ((0, 32), (1, 8))),
        "panel": normal_values(seeds[1], (R, NS, W), (R // 2) ** -0.5, 0.0625, ((0, 8), (2, 32))),
        "block_mask": with_ends((jax.random.randint(seeds[2], (NS, RB), 0, 2) < 1).astype(jnp.int32), jax.random.fold_in(seeds[2], 1), 0, 1),
        "diag_inverse": normal_values(seeds[3], (NS, W, W), 1.0, 6.0, ((1, 32), (2, 8)), jnp.float32),
    }


def reference(inverse_root, panel, block_mask, diag_inverse):
    mask_rows = jnp.repeat(block_mask, W, axis=1)
    masked = panel * jnp.transpose(mask_rows).astype(jnp.bfloat16)[:, :, None]
    product = jnp.dot(inverse_root, masked.reshape(R, NS * W), preferred_element_type=jnp.float32).reshape(R, NS, W)
    block_inverse = diag_inverse + jnp.einsum("rkv,rkw->kvw", masked.astype(jnp.float32), product, precision=lax.Precision.HIGHEST)
    return -product, block_inverse
```

```python
import functools

import jax
import jax.numpy as jnp
from jax import lax
from jax.experimental import pallas as pl
from jax.experimental.pallas import tpu as pltpu
from jax.sharding import Mesh, PartitionSpec as P

CHUNKS = (4, 4)
SCALE = 64.0
NT = (((1,), (1,)), ((), ()))
VMEM = pl.BlockSpec(memory_space=pltpu.VMEM)
SMEM = pl.BlockSpec(memory_space=pltpu.SMEM)


def product_kernel(rows, ids, own, fwd, bwd, far_a, far_b, weights, select, out, picked, gathered, pair):
    ix, iz = ids[0], ids[1]

    def place(piece, first, count, x):
        for s in range(count):
            z = lax.rem(iz + 4 - (first + s), 4)
            start = pl.multiple_of((x * 4 + z) * rows, 16)
            gathered[pl.ds(start, rows), :] = piece[s * rows:(s + 1) * rows, :]

    place(own, 0, 4, ix)
    place(fwd, 0, 4, lax.rem(ix + 3, 4))
    place(bwd, 0, 4, lax.rem(ix + 1, 4))
    place(far_a, 0, 2, lax.rem(ix + 2, 4))
    place(far_b, 2, 2, lax.rem(ix + 2, 4))
    for t in range(4):
        pair[0:128, :] = weights[2 * t]
        pair[128:256, :] = weights[2 * t + 1]
        prod = lax.dot_general(gathered[...], pair[...], NT, preferred_element_type=jnp.float32)
        out[2 * t] = prod[:, 0:128]
        out[2 * t + 1] = prod[:, 128:256]
    picked[...] = lax.dot_general(
        gathered[...], select[...], NT, preferred_element_type=jnp.float32
    ).astype(picked.dtype)


def product_call(kc, ids, own, fwd, bwd, far_a, far_b, weights, select):
    n = 128 * kc
    return pl.pallas_call(
        functools.partial(product_kernel, 8 * kc),
        out_shape=(
            jax.ShapeDtypeStruct((8, n, 128), jnp.float32),
            jax.ShapeDtypeStruct((n, 128), jnp.bfloat16),
        ),
        in_specs=[SMEM] + [VMEM] * 7,
        out_specs=(VMEM, VMEM),
        scratch_shapes=[pltpu.VMEM((n, 2048), jnp.bfloat16), pltpu.VMEM((256, 2048), jnp.bfloat16)],
        compiler_params=pltpu.CompilerParams(vmem_limit_bytes=40 * 2**20),
        cost_estimate=pl.CostEstimate(flops=2 * n * 2048 * 1152, bytes_accessed=2 * n * 2048 + 10 * 2**20, transcendentals=0),
    )(ids, own, fwd, bwd, far_a, far_b, weights, select)


def diag_kernel(kc, product, mine, other, keep, give, diag):
    total = product[...].reshape(16, kc, 8, 128)
    left = mine[...].astype(jnp.float32).reshape(16, kc, 8, 128)
    right = pltpu.roll(other[...].astype(jnp.float32), 64, 1).reshape(16, kc, 8, 128)
    low = lax.broadcasted_iota(jnp.int32, (128, 128), 1) < 64
    per_k = [total[:, k].reshape(128, 128) for k in range(kc)]
    for t in range(kc // 2):
        a, b = per_k[2 * t], per_k[2 * t + 1]
        keep[t] = -jnp.where(low, a, pltpu.roll(b, 64, 1))
        give[t] = -jnp.where(low, pltpu.roll(a, 64, 1), b)
    for k in range(kc):
        p = per_k[k]
        hi = p.astype(jnp.bfloat16)
        rest = p - hi.astype(jnp.float32)
        mid = rest.astype(jnp.bfloat16)
        lo = (rest - mid.astype(jnp.float32)).astype(jnp.bfloat16)
        m = jnp.concatenate([left[:, k].reshape(128, 128), right[:, k].reshape(128, 128)], axis=0).astype(jnp.bfloat16)
        d = lax.dot_general(lo, m, NT, preferred_element_type=jnp.float32)
        d += lax.dot_general(mid, m, NT, preferred_element_type=jnp.float32)
        d += lax.dot_general(hi, m, NT, preferred_element_type=jnp.float32)
        for j in range(8):
            diag[j, k * 16:(k + 1) * 16, :] = d[j * 16:(j + 1) * 16, :]


def diag_call(kc, product, mine, other):
    return pl.pallas_call(
        functools.partial(diag_kernel, kc),
        out_shape=(
            jax.ShapeDtypeStruct((kc // 2, 128, 128), jnp.float32),
            jax.ShapeDtypeStruct((kc // 2, 128, 128), jnp.float32),
            jax.ShapeDtypeStruct((8, kc * 16, 256), jnp.float32),
        ),
        in_specs=[VMEM] * 3,
        out_specs=(VMEM,) * 3,
        compiler_params=pltpu.CompilerParams(vmem_limit_bytes=32 * 2**20),
        cost_estimate=pl.CostEstimate(flops=2 * kc * 3 * 128 * 128 * 256, bytes_accessed=8 * kc * 2**18, transcendentals=0),
    )(product, mine, other)


def rows_kernel(count, ids, *refs):
    keeps, gots, out = refs[:count], refs[count:2 * count], refs[2 * count]
    first = ids[2] == 0
    pair = 0
    for keep, got in zip(keeps, gots):
        for t in range(keep.shape[0]):
            a, b = keep[t].reshape(16, 1, 8, 128), got[t].reshape(16, 1, 8, 128)
            even, odd = jnp.where(first, a, b), jnp.where(first, b, a)
            both = jnp.concatenate([even, odd], axis=1).reshape(256, 128).T
            out[:, 2 * pair, :] = both[0:64, :]
            out[:, 2 * pair + 1, :] = both[64:128, :]
            pair += 1


def rows_call(ids, keeps, gots):
    return pl.pallas_call(
        functools.partial(rows_kernel, len(keeps)),
        out_shape=jax.ShapeDtypeStruct((64, 8, 256), jnp.float32),
        in_specs=[SMEM] + [VMEM] * (2 * len(keeps)),
        out_specs=VMEM,
        compiler_params=pltpu.CompilerParams(vmem_limit_bytes=32 * 2**20),
        cost_estimate=pl.CostEstimate(flops=0, bytes_accessed=2**20, transcendentals=0),
    )(ids, *keeps, *gots)


def turn(size, shift):
    return [(i, (i + shift) % size) for i in range(size)]


def owner_route():
    route = []
    for x in range(4):
        for z in range(4):
            for low in range(2):
                for y in range(4):
                    row = 2 * (low * 4 + y) + z // 2
                    source = ((x * 4 + z) * 2 + low) * 4 + y
                    route.append((source, (row * 2 + z % 2) * 4 + x))
    return route


def shards(inverse_root, panel, block_mask, diag_inverse):
    ix, iz, ic = lax.axis_index("x"), lax.axis_index("zh"), lax.axis_index("core")
    col = lax.axis_index("zl") * 4 + lax.axis_index("y")
    ids = jnp.stack([ix, iz, ic]).astype(jnp.int32)
    swap = [(0, 1), (1, 0)]

    mask_here = lax.dynamic_slice_in_dim(block_mask, col * 8, 8, 1).astype(jnp.bfloat16)
    masked = jnp.transpose(panel, (1, 2, 0)) * jnp.repeat(mask_here, 256, axis=1)[:, None, :]

    starts = [sum(CHUNKS[:i]) for i in range(len(CHUNKS))]
    slabs = []
    for first, kc in zip(starts, CHUNKS):
        own = masked[first:first + kc].reshape(kc * 8, 2048)
        slabs.append((own, [lax.ppermute(own, "zh", turn(4, s)) for s in (1, 2, 3)]))

    other_root = lax.ppermute(inverse_root, "core", swap)
    weights = jnp.concatenate([inverse_root.reshape(8, 64, 2048), other_root.reshape(8, 64, 2048)], axis=1)

    lane = lax.broadcasted_iota(jnp.int32, (128, 2048), 0)
    at = lax.broadcasted_iota(jnp.int32, (128, 2048), 1)
    wanted = (iz // 2) * 1024 + (ic ^ (lane // 64)) * 512 + ((iz % 2) * 4 + ix) * 64 + lane % 64
    select = (at == wanted).astype(jnp.bfloat16)

    keeps, gots, summed = [], [], []
    for (own, others), kc in zip(slabs, CHUNKS):
        half = 16 * kc
        slab = jnp.concatenate([own] + others, axis=0)
        fwd = lax.ppermute(slab, "x", turn(4, 1))
        bwd = lax.ppermute(slab, "x", turn(4, -1))
        far_a = lax.ppermute(fwd[:half], "x", turn(4, 1))
        far_b = lax.ppermute(bwd[half:], "x", turn(4, -1))
        partial, picked = product_call(kc, ids, slab, fwd, bwd, far_a, far_b, weights, select)
        mine = lax.ppermute(picked, ("x", "zh", "zl", "y"), owner_route())
        other = lax.ppermute(mine, "core", swap)
        sent = (partial * SCALE).astype(jnp.float16)
        parts = lax.all_to_all(sent, ("zl", "y"), 0, 0, tiled=True)
        product = jnp.sum(parts.astype(jnp.float32), axis=0) * (1.0 / SCALE)
        keep, give, diag = diag_call(kc, product, mine, other)
        keeps.append(keep)
        gots.append(lax.ppermute(give, "core", swap))
        summed.append(jnp.sum(lax.all_to_all(diag, ("zl", "y"), 0, 0, tiled=True), axis=0))

    panel_inverse = rows_call(ids, keeps, gots)

    across = jnp.concatenate(summed, axis=0).T.reshape(2, 16, 8, 128)
    across = jnp.transpose(across, (1, 0, 2, 3))
    here = jnp.sum(lax.all_to_all(across, ("x", "zh"), 0, 0, tiled=True), axis=0)
    came = lax.ppermute(here[1], "core", swap)
    even, odd = jnp.where(ic == 0, here[0], came), jnp.where(ic == 0, came, here[0])
    both = jnp.stack([even.reshape(8, 8, 2, 8), odd.reshape(8, 8, 2, 8)], axis=3)
    block = jnp.transpose(both, (1, 0, 2, 3, 4)).reshape(8, 8, 32)
    return panel_inverse, diag_inverse + block


def solution(mesh):
    wide = Mesh(mesh.devices.reshape(4, 4, 2, 2, 4), ("x", "zh", "core", "zl", "y"))
    prow, pcol = ("x", "zh", "core"), ("zl", "y")
    in_specs = (P(prow, pcol), P(pcol, None, prow), P(), P(None, prow, pcol))
    out_specs = (P(prow + pcol, None, None), P(None, prow, pcol))
    return jax.shard_map(shards, mesh=wide, in_specs=in_specs, out_specs=out_specs, check_vma=False)
```

```python
import functools

import jax
import jax.numpy as jnp
from jax import lax
from jax.experimental import pallas as pl
from jax.experimental.pallas import tpu as pltpu
from jax.sharding import Mesh, PartitionSpec as P

GROUPS = ((0,), (1, 3, 2))
SCALE = 64.0
NT = (((1,), (1,)), ((), ()))
VMEM = pl.BlockSpec(memory_space=pltpu.VMEM)
ANY = pl.BlockSpec(memory_space=pl.ANY)
SMEM = pl.BlockSpec(memory_space=pltpu.SMEM)


def mask_kernel(ids, mask, panel, own, pieces):
    ic, col = ids[2], ids[3]
    upper = lax.broadcasted_iota(jnp.int32, (16, 256), 0) < 8
    low = lax.broadcasted_iota(jnp.int32, (16, 128), 1) < 64
    for t in range(4):
        rows = slice(16 * t, 16 * t + 16)
        blocks = []
        for i in range(8):
            lanes = slice(256 * i, 256 * i + 256)
            here = jnp.where(upper, mask[2 * t, col * 8 + i], mask[2 * t + 1, col * 8 + i]).astype(jnp.float32)
            blocks.append(panel[rows, lanes].astype(jnp.float32) * here)
            own[rows, lanes] = blocks[-1].astype(own.dtype)
        for b in range(2):
            for h in range(2):
                even, odd = blocks[4 * b + h], blocks[4 * b + 2 + h]
                first, second = jnp.where(ic == 0, even, odd), jnp.where(ic == 0, odd, even)
                for u in range(2):
                    p, q = first[:, 128 * u:128 * u + 128], second[:, 128 * u:128 * u + 128]
                    j = 4 * h + 2 * u
                    pieces[j, b, rows, :] = jnp.where(low, p, pltpu.roll(q, 64, 1)).astype(pieces.dtype)
                    pieces[j + 1, b, rows, :] = jnp.where(low, pltpu.roll(p, 64, 1), q).astype(pieces.dtype)


def mask_call(ids, mask, panel):
    return pl.pallas_call(
        mask_kernel,
        out_shape=(
            jax.ShapeDtypeStruct((64, 2048), jnp.bfloat16),
            jax.ShapeDtypeStruct((8, 2, 64, 128), jnp.bfloat16),
        ),
        in_specs=[SMEM, SMEM, VMEM],
        out_specs=(VMEM, VMEM),
        compiler_params=pltpu.CompilerParams(vmem_limit_bytes=16 * 2**20),
        cost_estimate=pl.CostEstimate(flops=1, bytes_accessed=2**20, transcendentals=0),
    )(ids, mask, panel)


def product_kernel(places, size, ids, *refs):
    count = len(places)
    slabs, (root, other_root, out, gathered, pair) = refs[:count], refs[count:]

    @pl.when(pl.program_id(0) == 0)
    def _():
        for slab, (shift, skip) in zip(slabs, places):
            start = pl.multiple_of(lax.rem(ids[0] + shift, 4) * size + skip, 16)
            gathered[pl.ds(start, slab.shape[0]), :] = slab[...]

    for j in range(2):
        pair[128 * j:128 * j + 64, :] = root[64 * j:64 * j + 64, :]
        pair[128 * j + 64:128 * j + 128, :] = other_root[64 * j:64 * j + 64, :]
    prod = lax.dot_general(gathered[...], pair[...], NT, preferred_element_type=jnp.float32)
    out[0] = prod[:, 0:128] * SCALE
    out[1] = prod[:, 128:256] * SCALE


def product_call(ids, slabs, places, size, root, other_root):
    n = 4 * size
    return pl.pallas_call(
        functools.partial(product_kernel, places, size),
        grid=(4,),
        out_shape=jax.ShapeDtypeStruct((8, n, 128), jnp.float32),
        in_specs=[SMEM] + [pl.BlockSpec(slab.shape, lambda t: (0, 0)) for slab in slabs]
        + [pl.BlockSpec((128, 2048), lambda t: (t, 0))] * 2,
        out_specs=pl.BlockSpec((2, n, 128), lambda t: (t, 0, 0)),
        scratch_shapes=[pltpu.VMEM((n, 2048), jnp.bfloat16), pltpu.VMEM((256, 2048), jnp.bfloat16)],
        compiler_params=pltpu.CompilerParams(vmem_limit_bytes=24 * 2**20),
        cost_estimate=pl.CostEstimate(flops=2 * n * 2048 * 1024, bytes_accessed=2 * n * 2048 + 6 * 2**20, transcendentals=0),
    )(ids, *slabs, root, other_root)


def diag_kernel(ids, *refs):
    count = len(GROUPS)
    products, (mine, other, keep, give, diag) = refs[:count], refs[count:]
    iz = ids[1]
    low = lax.broadcasted_iota(jnp.int32, (8, 128), 1) < 64
    left = mine[...].astype(jnp.float32).reshape(16, 8, 8, 128)
    right = pltpu.roll(other[...].astype(jnp.float32), 64, 2).reshape(16, 8, 8, 128)
    totals, places = [], []
    for product, group in zip(products, GROUPS):
        total = product[...].reshape(4, len(group), 8, 8, 128)
        for q, s in enumerate(group):
            z = lax.rem(iz + 4 - s, 4)
            for x in range(4):
                totals.append(total[x, q])
                places.append((x, z))
                for t in range(4):
                    even, odd = total[x, q, 2 * t], total[x, q, 2 * t + 1]
                    keep[t, x, z] = -jnp.where(low, even, pltpu.roll(odd, 64, 1))
                    give[t, x, z] = -jnp.where(low, pltpu.roll(even, 64, 1), odd)
    for k in range(8):
        p = jnp.concatenate([total[k] for total in totals], axis=0)
        hi = p.astype(jnp.bfloat16)
        rest = p - hi.astype(jnp.float32)
        mid = rest.astype(jnp.bfloat16)
        lo = (rest - mid.astype(jnp.float32)).astype(jnp.bfloat16)
        m = jnp.concatenate([left[:, k].reshape(128, 128), right[:, k].reshape(128, 128)], axis=0).astype(jnp.bfloat16)
        d = lax.dot_general(lo, m, NT, preferred_element_type=jnp.float32)
        d += lax.dot_general(mid, m, NT, preferred_element_type=jnp.float32)
        d += lax.dot_general(hi, m, NT, preferred_element_type=jnp.float32)
        for i, (x, z) in enumerate(places):
            diag[2 * x + z // 2, k, lax.rem(z, 2)] = d[i * 8:(i + 1) * 8, :]


def diag_call(ids, products, mine, other):
    return pl.pallas_call(
        diag_kernel,
        out_shape=(
            jax.ShapeDtypeStruct((4, 4, 4, 8, 128), jnp.float32),
            jax.ShapeDtypeStruct((4, 4, 4, 8, 128), jnp.float32),
            jax.ShapeDtypeStruct((8, 8, 2, 8, 256), jnp.float32),
        ),
        in_specs=[SMEM] + [VMEM] * (len(GROUPS) + 2),
        out_specs=(VMEM,) * 3,
        compiler_params=pltpu.CompilerParams(vmem_limit_bytes=16 * 2**20),
        cost_estimate=pl.CostEstimate(flops=2 * 8 * 3 * 128 * 128 * 256, bytes_accessed=2**23, transcendentals=0),
    )(ids, *products, mine, other)


def rows_kernel(ids, keep, got, out):
    first = ids[2] == 0
    for t in range(4):
        a, b = keep[t].reshape(16, 1, 8, 128), got[t].reshape(16, 1, 8, 128)
        even, odd = jnp.where(first, a, b), jnp.where(first, b, a)
        both = jnp.concatenate([even, odd], axis=1).reshape(256, 128).T
        out[:, 2 * t, :] = both[0:64, :]
        out[:, 2 * t + 1, :] = both[64:128, :]


def rows_call(ids, keep, got):
    return pl.pallas_call(
        rows_kernel,
        out_shape=jax.ShapeDtypeStruct((64, 8, 256), jnp.float32),
        in_specs=[SMEM, VMEM, VMEM],
        out_specs=VMEM,
        compiler_params=pltpu.CompilerParams(vmem_limit_bytes=16 * 2**20),
        cost_estimate=pl.CostEstimate(flops=0, bytes_accessed=2**20, transcendentals=0),
    )(ids, keep, got)


def pin(values):
    return lax.optimization_barrier(values)


def turn(size, shift):
    return [(i, (i + shift) % size) for i in range(size)]


def shards(inverse_root, panel, block_mask, diag_inverse):
    ix, iz, ic = lax.axis_index("x"), lax.axis_index("zh"), lax.axis_index("core")
    col = lax.axis_index("zl") * 4 + lax.axis_index("y")
    ids = jnp.stack([ix, iz, ic, col]).astype(jnp.int32)
    swap = [(0, 1), (1, 0)]

    def sum_parts(parts):
        return jnp.sum(parts.astype(jnp.float32), axis=0) * (1.0 / SCALE)

    def send_parts(partial):
        return partial.astype(jnp.float16)

    def around(slab):
        return [lax.ppermute(slab, "x", turn(4, 1)), lax.ppermute(slab, "x", turn(4, -1))]

    def to_columns(value):
        return lax.all_to_all(value, ("zl", "y"), 0, 0, tiled=True)

    def to_rows(value):
        return lax.all_to_all(value, ("x", "zh"), 0, 0, tiled=True)

    other_root = lax.ppermute(inverse_root, "core", swap)
    own, pieces = mask_call(ids, block_mask, jnp.transpose(panel, (1, 2, 0)).reshape(64, 2048))

    z1, z3 = (lax.ppermute(own, "zh", turn(4, s)) for s in (1, 3))
    near0, pieces = pin((around(own), pieces))
    far0 = lax.ppermute(near0[0], "x", turn(4, 1))
    pieces = to_columns(pieces)
    z1, z3, near0, far0, own, other_root = pin((z1, z3, near0, far0, own, other_root))

    z2 = lax.ppermute(own, "zh", turn(4, 2))
    near1, near3 = around(z1), around(z3)
    sent0 = send_parts(
        product_call(ids, [own, *near0, far0], [(0, 0), (3, 0), (1, 0), (2, 0)], 64, inverse_root, other_root)
    )
    z2, near1, near3, pieces, sent0 = pin((z2, near1, near3, pieces, sent0))

    far1, far3 = lax.ppermute(near1[0], "x", turn(4, 1)), lax.ppermute(near3[1], "x", turn(4, -1))
    near2 = around(z2)
    far1, sent0 = pin((far1, sent0))
    parts0 = to_columns(sent0)
    far1, far3, near2 = pin((far1, far3, near2))

    far2 = [lax.ppermute(near2[0][:32], "x", turn(4, 1)), lax.ppermute(near2[1][32:], "x", turn(4, -1))]
    far2, pieces, parts0 = pin((far2, pieces, parts0))

    sent1 = send_parts(product_call(
        ids,
        [z1, *near1, far1, z3, *near3, far3, z2, *near2, *far2],
        [(0, 0), (3, 0), (1, 0), (2, 0), (0, 64), (3, 64), (1, 64), (2, 64), (0, 128), (3, 128), (1, 128), (2, 128), (2, 160)],
        192, inverse_root, other_root,
    ))
    parts1 = to_columns(sent1)
    mine = to_rows(pieces.reshape(16, 64, 128))
    other = lax.ppermute(mine, "core", swap)
    products = [sum_parts(parts0), sum_parts(parts1)]

    keep, give, diag = diag_call(ids, products, mine, other)
    got = lax.ppermute(give, "core", swap)
    here = jnp.sum(to_columns(diag), axis=0)
    panel_inverse = rows_call(ids, keep, got)
    here, panel_inverse = lax.optimization_barrier((here, panel_inverse))
    across = here.reshape(128, 256).T.reshape(2, 16, 8, 128)
    across = jnp.transpose(across, (1, 0, 2, 3))
    here = jnp.sum(to_rows(across), axis=0)
    came = lax.ppermute(here[1], "core", swap)
    even, odd = jnp.where(ic == 0, here[0], came), jnp.where(ic == 0, came, here[0])
    both = jnp.stack([even.reshape(8, 8, 2, 8), odd.reshape(8, 8, 2, 8)], axis=3)
    block = jnp.transpose(both, (1, 0, 2, 3, 4)).reshape(8, 8, 32)
    return panel_inverse, diag_inverse + block


def solution(mesh):
    wide = Mesh(mesh.devices.reshape(4, 4, 2, 2, 4), ("x", "zh", "core", "zl", "y"))
    prow, pcol = ("x", "zh", "core"), ("zl", "y")
    in_specs = (P(prow, pcol), P(pcol, None, prow), P(), P(None, prow, pcol))
    out_specs = (P(prow + pcol, None, None), P(None, prow, pcol))
    return jax.shard_map(shards, mesh=wide, in_specs=in_specs, out_specs=out_specs, check_vma=False)
```

```python
import functools

import jax
import jax.numpy as jnp
from jax import lax
from jax.experimental import pallas as pl
from jax.experimental.pallas import tpu as pltpu
from jax.sharding import Mesh, PartitionSpec as P

EARLY = ((0, 0), (3, 0), (1, 0), (2, 0), (0, 1), (3, 1), (1, 1), (0, 3), (3, 3), (1, 3))
LATE = ((2, 1), (2, 3), (0, 2), (3, 2), (1, 2), (2, 2))
SCALE = 64.0
NT = (((1,), (1,)), ((), ()))
VMEM = pl.BlockSpec(memory_space=pltpu.VMEM)
ANY = pl.BlockSpec(memory_space=pl.ANY)
SMEM = pl.BlockSpec(memory_space=pltpu.SMEM)


def mask_kernel(ids, mask, panel, own, pieces):
    ic, col = ids[2], ids[3]
    upper = lax.broadcasted_iota(jnp.int32, (16, 256), 0) < 8
    low = lax.broadcasted_iota(jnp.int32, (16, 128), 1) < 64
    for t in range(4):
        rows = slice(16 * t, 16 * t + 16)
        blocks = []
        for i in range(8):
            lanes = slice(256 * i, 256 * i + 256)
            here = jnp.where(upper, mask[2 * t, col * 8 + i], mask[2 * t + 1, col * 8 + i]).astype(jnp.float32)
            blocks.append(panel[rows, lanes].astype(jnp.float32) * here)
            own[rows, lanes] = blocks[-1].astype(own.dtype)
        for b in range(2):
            for h in range(2):
                even, odd = blocks[4 * b + h], blocks[4 * b + 2 + h]
                first, second = jnp.where(ic == 0, even, odd), jnp.where(ic == 0, odd, even)
                for u in range(2):
                    p, q = first[:, 128 * u:128 * u + 128], second[:, 128 * u:128 * u + 128]
                    j = 4 * h + 2 * u
                    pieces[j, b, rows, :] = jnp.where(low, p, pltpu.roll(q, 64, 1)).astype(pieces.dtype)
                    pieces[j + 1, b, rows, :] = jnp.where(low, pltpu.roll(p, 64, 1), q).astype(pieces.dtype)


def mask_call(ids, mask, panel):
    return pl.pallas_call(
        mask_kernel,
        out_shape=(
            jax.ShapeDtypeStruct((64, 2048), jnp.bfloat16),
            jax.ShapeDtypeStruct((8, 2, 64, 128), jnp.bfloat16),
        ),
        in_specs=[SMEM, SMEM, VMEM],
        out_specs=(VMEM, VMEM),
        compiler_params=pltpu.CompilerParams(vmem_limit_bytes=16 * 2**20),
        cost_estimate=pl.CostEstimate(flops=1, bytes_accessed=2**20, transcendentals=0),
    )(ids, mask, panel)


def product_kernel(ids, *refs):
    slabs, (root, other_root, out, gathered, pair) = refs[:-5], refs[-5:]

    @pl.when(pl.program_id(0) == 0)
    def _():
        start = 0
        for slab in slabs:
            gathered[start:start + slab.shape[0], :] = slab[...]
            start += slab.shape[0]

    for j in range(2):
        pair[128 * j:128 * j + 64, :] = root[64 * j:64 * j + 64, :]
        pair[128 * j + 64:128 * j + 128, :] = other_root[64 * j:64 * j + 64, :]
    prod = lax.dot_general(gathered[...], pair[...], NT, preferred_element_type=jnp.float32)
    out[0] = prod[:, 0:128] * SCALE
    out[1] = prod[:, 128:256] * SCALE


def product_call(ids, slabs, root, other_root, vmem):
    n = sum(slab.shape[0] for slab in slabs)
    return pl.pallas_call(
        product_kernel,
        grid=(4,),
        out_shape=jax.ShapeDtypeStruct((8, n, 128), jnp.float32),
        in_specs=[SMEM] + [pl.BlockSpec(slab.shape, lambda t: (0, 0)) for slab in slabs]
        + [pl.BlockSpec((128, 2048), lambda t: (t, 0))] * 2,
        out_specs=pl.BlockSpec((2, n, 128), lambda t: (t, 0, 0)),
        scratch_shapes=[pltpu.VMEM((n, 2048), jnp.bfloat16), pltpu.VMEM((256, 2048), jnp.bfloat16)],
        compiler_params=pltpu.CompilerParams(vmem_limit_bytes=vmem * 2**20),
        cost_estimate=pl.CostEstimate(flops=2 * n * 2048 * 1024, bytes_accessed=2 * n * 2048 + 6 * 2**20, transcendentals=0),
    )(ids, *slabs, root, other_root)


def mark_kernel(source, out):
    out[...] = jnp.zeros_like(out)


def mark_call(value):
    return pl.pallas_call(
        mark_kernel,
        out_shape=jax.ShapeDtypeStruct((8, 128), jnp.float32),
        in_specs=[ANY],
        out_specs=VMEM,
        cost_estimate=pl.CostEstimate(flops=2**34, bytes_accessed=2**12, transcendentals=0),
    )(value)


def hold_kernel(after, source, out):
    out[...] = source[...]


def hold_call(after, value):
    return pl.pallas_call(
        hold_kernel,
        out_shape=jax.ShapeDtypeStruct(value.shape, value.dtype),
        in_specs=[ANY, VMEM],
        out_specs=VMEM,
        cost_estimate=pl.CostEstimate(flops=2**34, bytes_accessed=2**19, transcendentals=0),
    )(after, value)


def diag_kernel(ids, early, late, mine, other, keep, give, diag):
    ix, iz = ids[0], ids[1]
    low = lax.broadcasted_iota(jnp.int32, (8, 128), 1) < 64
    left = mine[...].astype(jnp.float32).reshape(16, 8, 8, 128)
    right = pltpu.roll(other[...].astype(jnp.float32), 64, 2).reshape(16, 8, 8, 128)
    totals, places = [], []
    slabs = [early[64 * i:64 * i + 64, :] for i in range(len(EARLY))] + [late[64 * i:64 * i + 64, :] for i in range(len(LATE))]
    for slab, (dx, dz) in zip(slabs, EARLY + LATE):
        total = slab.reshape(8, 8, 128)
        x, z = lax.rem(ix + dx, 4), lax.rem(iz + 4 - dz, 4)
        totals.append(total)
        places.append((2 * x + lax.div(z, 2), lax.rem(z, 2)))
        for t in range(4):
            even, odd = total[2 * t], total[2 * t + 1]
            keep[t, x, z] = -jnp.where(low, even, pltpu.roll(odd, 64, 1))
            give[t, x, z] = -jnp.where(low, pltpu.roll(even, 64, 1), odd)
    for k in range(8):
        p = jnp.concatenate([total[k] for total in totals], axis=0)
        hi = p.astype(jnp.bfloat16)
        rest = p - hi.astype(jnp.float32)
        mid = rest.astype(jnp.bfloat16)
        lo = (rest - mid.astype(jnp.float32)).astype(jnp.bfloat16)
        m = jnp.concatenate([left[:, k].reshape(128, 128), right[:, k].reshape(128, 128)], axis=0).astype(jnp.bfloat16)
        d = lax.dot_general(lo, m, NT, preferred_element_type=jnp.float32)
        d += lax.dot_general(mid, m, NT, preferred_element_type=jnp.float32)
        d += lax.dot_general(hi, m, NT, preferred_element_type=jnp.float32)
        for i, (column, z) in enumerate(places):
            diag[column, k, z] = d[i * 8:(i + 1) * 8, :]


def diag_call(ids, early, late, mine, other):
    return pl.pallas_call(
        diag_kernel,
        out_shape=(
            jax.ShapeDtypeStruct((4, 4, 4, 8, 128), jnp.float32),
            jax.ShapeDtypeStruct((4, 4, 4, 8, 128), jnp.float32),
            jax.ShapeDtypeStruct((8, 8, 2, 8, 256), jnp.float32),
        ),
        in_specs=[SMEM] + [VMEM] * 4,
        out_specs=(VMEM,) * 3,
        compiler_params=pltpu.CompilerParams(vmem_limit_bytes=16 * 2**20),
        cost_estimate=pl.CostEstimate(flops=2 * 8 * 3 * 128 * 128 * 256, bytes_accessed=2**23, transcendentals=0),
    )(ids, early, late, mine, other)


def rows_kernel(ids, keep, got, out):
    first = ids[2] == 0
    for t in range(4):
        a, b = keep[t].reshape(16, 1, 8, 128), got[t].reshape(16, 1, 8, 128)
        even, odd = jnp.where(first, a, b), jnp.where(first, b, a)
        both = jnp.concatenate([even, odd], axis=1).reshape(256, 128).T
        out[:, 2 * t, :] = both[0:64, :]
        out[:, 2 * t + 1, :] = both[64:128, :]


def rows_call(ids, keep, got):
    return pl.pallas_call(
        rows_kernel,
        out_shape=jax.ShapeDtypeStruct((64, 8, 256), jnp.float32),
        in_specs=[SMEM, VMEM, VMEM],
        out_specs=VMEM,
        compiler_params=pltpu.CompilerParams(vmem_limit_bytes=16 * 2**20),
        cost_estimate=pl.CostEstimate(flops=0, bytes_accessed=2**20, transcendentals=0),
    )(ids, keep, got)


def pin(values):
    return lax.optimization_barrier(values)


def turn(size, shift):
    return [(i, (i + shift) % size) for i in range(size)]


def shards(inverse_root, panel, block_mask, diag_inverse):
    ix, iz, ic = lax.axis_index("x"), lax.axis_index("zh"), lax.axis_index("core")
    col = lax.axis_index("zl") * 4 + lax.axis_index("y")
    ids = jnp.stack([ix, iz, ic, col]).astype(jnp.int32)
    swap = [(0, 1), (1, 0)]

    def sum_parts(parts):
        return jnp.sum(parts.astype(jnp.float32), axis=0) * (1.0 / SCALE)

    def send_parts(partial):
        return partial.astype(jnp.float16)

    def around(slab):
        return [lax.ppermute(slab, "x", turn(4, 1)), lax.ppermute(slab, "x", turn(4, -1))]

    def to_columns(value):
        return lax.all_to_all(value, ("zl", "y"), 0, 0, tiled=True)

    def to_rows(value):
        return lax.all_to_all(value, ("x", "zh"), 0, 0, tiled=True)

    other_root = lax.ppermute(inverse_root, "core", swap)
    own, pieces = mask_call(ids, block_mask, jnp.transpose(panel, (1, 2, 0)).reshape(64, 2048))

    z1, z3 = (lax.ppermute(own, "zh", turn(4, s)) for s in (1, 3))
    near0, pieces = pin((around(own), pieces))
    far0 = lax.ppermute(near0[0], "x", turn(4, 1))
    pieces = to_columns(pieces)
    z1, z3, near0, far0, own, other_root = pin((z1, z3, near0, far0, own, other_root))

    z2 = lax.ppermute(own, "zh", turn(4, 2))
    near1, near3 = around(z1), around(z3)
    mine = to_rows(hold_call(mark_call(own), pieces.reshape(16, 64, 128)))
    z2, near1, near3 = pin((z2, near1, near3))

    far1, far3 = lax.ppermute(near1[0], "x", turn(4, 1)), lax.ppermute(near3[1], "x", turn(4, -1))
    near2 = around(z2)
    early = send_parts(product_call(ids, [own, *near0, far0, z1, *near1, z3, *near3], inverse_root, other_root, 58))
    far1, far3, near2, early, mine = pin((far1, far3, near2, early, mine))

    parts = to_columns(early)
    far2 = lax.ppermute(near2[0], "x", turn(4, 1))
    far2 = pin((far2,))[0]

    late = send_parts(product_call(ids, [far1, far3, z2, *near2, far2], inverse_root, other_root, 24))
    late, parts = pin((late, parts))
    other = lax.ppermute(mine, "core", swap)
    keep, give, diag = diag_call(ids, sum_parts(parts), sum_parts(to_columns(late)), mine, other)
    got = lax.ppermute(give, "core", swap)
    here = jnp.sum(to_columns(diag), axis=0)
    panel_inverse = rows_call(ids, keep, got)
    here, panel_inverse = lax.optimization_barrier((here, panel_inverse))
    across = here.reshape(128, 256).T.reshape(2, 16, 8, 128)
    across = jnp.transpose(across, (1, 0, 2, 3))
    here = jnp.sum(to_rows(across), axis=0)
    came = lax.ppermute(here[1], "core", swap)
    even, odd = jnp.where(ic == 0, here[0], came), jnp.where(ic == 0, came, here[0])
    both = jnp.stack([even.reshape(8, 8, 2, 8), odd.reshape(8, 8, 2, 8)], axis=3)
    block = jnp.transpose(both, (1, 0, 2, 3, 4)).reshape(8, 8, 32)
    return panel_inverse, diag_inverse + block


def solution(mesh):
    wide = Mesh(mesh.devices.reshape(4, 4, 2, 2, 4), ("x", "zh", "core", "zl", "y"))
    prow, pcol = ("x", "zh", "core"), ("zl", "y")
    in_specs = (P(prow, pcol), P(pcol, None, prow), P(), P(None, prow, pcol))
    out_specs = (P(prow + pcol, None, None), P(None, prow, pcol))
    return jax.shard_map(shards, mesh=wide, in_specs=in_specs, out_specs=out_specs, check_vma=False)
```

```python
import functools

import jax
import jax.numpy as jnp
from jax import lax
from jax.experimental import pallas as pl
from jax.experimental.pallas import tpu as pltpu
from jax.sharding import Mesh, PartitionSpec as P

EARLY = ((0, 0), (3, 0), (1, 0), (2, 0), (0, 1), (3, 1), (1, 1), (0, 3), (3, 3), (1, 3))
LATE = ((2, 1), (2, 3), (0, 2), (3, 2), (1, 2), (2, 2))
SCALE = 64.0
NT = (((1,), (1,)), ((), ()))
VMEM = pl.BlockSpec(memory_space=pltpu.VMEM)
ANY = pl.BlockSpec(memory_space=pl.ANY)
SMEM = pl.BlockSpec(memory_space=pltpu.SMEM)


def mask_kernel(ids, mask, panel, own, pieces):
    ic, col, t = ids[2], ids[3], pl.program_id(0)
    upper = lax.broadcasted_iota(jnp.int32, (16, 256), 0) < 8
    low = lax.broadcasted_iota(jnp.int32, (16, 128), 1) < 64
    blocks = []
    for i in range(8):
        lanes = slice(256 * i, 256 * i + 256)
        here = jnp.where(upper, mask[2 * t, col * 8 + i], mask[2 * t + 1, col * 8 + i]).astype(jnp.float32)
        blocks.append(panel[:, lanes].astype(jnp.float32) * here)
        own[:, lanes] = blocks[-1].astype(own.dtype)
    for b in range(2):
        for h in range(2):
            even, odd = blocks[4 * b + h], blocks[4 * b + 2 + h]
            first, second = jnp.where(ic == 0, even, odd), jnp.where(ic == 0, odd, even)
            for u in range(2):
                p, q = first[:, 128 * u:128 * u + 128], second[:, 128 * u:128 * u + 128]
                j = 4 * h + 2 * u
                pieces[j, b] = jnp.where(low, p, pltpu.roll(q, 64, 1)).astype(pieces.dtype)
                pieces[j + 1, b] = jnp.where(low, pltpu.roll(p, 64, 1), q).astype(pieces.dtype)


def mask_call(ids, mask, panel):
    return pl.pallas_call(
        mask_kernel,
        grid=(4,),
        out_shape=(
            jax.ShapeDtypeStruct((64, 2048), jnp.bfloat16),
            jax.ShapeDtypeStruct((8, 2, 64, 128), jnp.bfloat16),
        ),
        in_specs=[SMEM, SMEM, pl.BlockSpec((16, 2048), lambda t: (t, 0))],
        out_specs=(
            pl.BlockSpec((16, 2048), lambda t: (t, 0)),
            pl.BlockSpec((8, 2, 16, 128), lambda t: (0, 0, t, 0)),
        ),
        compiler_params=pltpu.CompilerParams(vmem_limit_bytes=60 * 2**20),
        cost_estimate=pl.CostEstimate(flops=1, bytes_accessed=2**20, transcendentals=0),
    )(ids, mask, panel)


def product_kernel(ids, *refs):
    slabs, (root, other_root, out, gathered, pair) = refs[:-5], refs[-5:]

    @pl.when(pl.program_id(0) == 0)
    def _():
        start = 0
        for slab in slabs:
            gathered[start:start + slab.shape[0], :] = slab[...]
            start += slab.shape[0]

    for j in range(2):
        pair[128 * j:128 * j + 64, :] = root[64 * j:64 * j + 64, :]
        pair[128 * j + 64:128 * j + 128, :] = other_root[64 * j:64 * j + 64, :]
    prod = lax.dot_general(gathered[...], pair[...], NT, preferred_element_type=jnp.float32)
    out[0] = prod[:, 0:128] * SCALE
    out[1] = prod[:, 128:256] * SCALE


def product_call(ids, slabs, root, other_root, vmem):
    n = sum(slab.shape[0] for slab in slabs)
    return pl.pallas_call(
        product_kernel,
        grid=(4,),
        out_shape=jax.ShapeDtypeStruct((8, n, 128), jnp.float32),
        in_specs=[SMEM] + [pl.BlockSpec(slab.shape, lambda t: (0, 0)) for slab in slabs]
        + [pl.BlockSpec((128, 2048), lambda t: (t, 0))] * 2,
        out_specs=pl.BlockSpec((2, n, 128), lambda t: (t, 0, 0)),
        scratch_shapes=[pltpu.VMEM((n, 2048), jnp.bfloat16), pltpu.VMEM((256, 2048), jnp.bfloat16)],
        compiler_params=pltpu.CompilerParams(vmem_limit_bytes=vmem * 2**20),
        cost_estimate=pl.CostEstimate(flops=2 * n * 2048 * 1024, bytes_accessed=2 * n * 2048 + 6 * 2**20, transcendentals=0),
    )(ids, *slabs, root, other_root)


def mark_kernel(source, out):
    out[...] = jnp.zeros_like(out)


def mark_call(value):
    return pl.pallas_call(
        mark_kernel,
        out_shape=jax.ShapeDtypeStruct((8, 128), jnp.float32),
        in_specs=[ANY],
        out_specs=VMEM,
        cost_estimate=pl.CostEstimate(flops=2**34, bytes_accessed=2**12, transcendentals=0),
    )(value)


def hold_kernel(after, source, out):
    pass


def hold_call(after, value):
    return pl.pallas_call(
        hold_kernel,
        out_shape=jax.ShapeDtypeStruct(value.shape, value.dtype),
        in_specs=[ANY, ANY],
        out_specs=ANY,
        input_output_aliases={1: 0},
        cost_estimate=pl.CostEstimate(flops=2**34, bytes_accessed=2**12, transcendentals=0),
    )(after, value)


def diag_kernel(ids, early, late, mine, other, keep, give, diag):
    ix, iz = ids[0], ids[1]
    low = lax.broadcasted_iota(jnp.int32, (8, 128), 1) < 64
    left = mine[...].astype(jnp.float32).reshape(16, 8, 8, 128)
    right = pltpu.roll(other[...].astype(jnp.float32), 64, 2).reshape(16, 8, 8, 128)
    totals, places = [], []
    slabs = [early[64 * i:64 * i + 64, :] for i in range(len(EARLY))] + [late[64 * i:64 * i + 64, :] for i in range(len(LATE))]
    for slab, (dx, dz) in zip(slabs, EARLY + LATE):
        total = slab.reshape(8, 8, 128)
        x, z = lax.rem(ix + dx, 4), lax.rem(iz + 4 - dz, 4)
        totals.append(total)
        places.append((2 * x + lax.div(z, 2), lax.rem(z, 2)))
        for t in range(4):
            even, odd = total[2 * t], total[2 * t + 1]
            keep[t, x, z] = -jnp.where(low, even, pltpu.roll(odd, 64, 1))
            give[t, x, z] = -jnp.where(low, pltpu.roll(even, 64, 1), odd)
    for k in range(8):
        p = jnp.concatenate([total[k] for total in totals], axis=0)
        hi = p.astype(jnp.bfloat16)
        rest = p - hi.astype(jnp.float32)
        mid = rest.astype(jnp.bfloat16)
        lo = (rest - mid.astype(jnp.float32)).astype(jnp.bfloat16)
        m = jnp.concatenate([left[:, k].reshape(128, 128), right[:, k].reshape(128, 128)], axis=0).astype(jnp.bfloat16)
        d = lax.dot_general(lo, m, NT, preferred_element_type=jnp.float32)
        d += lax.dot_general(mid, m, NT, preferred_element_type=jnp.float32)
        d += lax.dot_general(hi, m, NT, preferred_element_type=jnp.float32)
        for i, (column, z) in enumerate(places):
            diag[column, k, z] = d[i * 8:(i + 1) * 8, :]


def diag_call(ids, early, late, mine, other):
    return pl.pallas_call(
        diag_kernel,
        out_shape=(
            jax.ShapeDtypeStruct((4, 4, 4, 8, 128), jnp.float32),
            jax.ShapeDtypeStruct((4, 4, 4, 8, 128), jnp.float32),
            jax.ShapeDtypeStruct((8, 8, 2, 8, 256), jnp.float32),
        ),
        in_specs=[SMEM] + [VMEM] * 4,
        out_specs=(VMEM,) * 3,
        compiler_params=pltpu.CompilerParams(vmem_limit_bytes=16 * 2**20),
        cost_estimate=pl.CostEstimate(flops=2 * 8 * 3 * 128 * 128 * 256, bytes_accessed=2**23, transcendentals=0),
    )(ids, early, late, mine, other)


def rows_kernel(ids, keep, got, out):
    first = ids[2] == 0
    for t in range(4):
        a, b = keep[t].reshape(16, 1, 8, 128), got[t].reshape(16, 1, 8, 128)
        even, odd = jnp.where(first, a, b), jnp.where(first, b, a)
        both = jnp.concatenate([even, odd], axis=1).reshape(256, 128).T
        out[:, 2 * t, :] = both[0:64, :]
        out[:, 2 * t + 1, :] = both[64:128, :]


def rows_call(ids, keep, got):
    return pl.pallas_call(
        rows_kernel,
        out_shape=jax.ShapeDtypeStruct((64, 8, 256), jnp.float32),
        in_specs=[SMEM, VMEM, VMEM],
        out_specs=VMEM,
        compiler_params=pltpu.CompilerParams(vmem_limit_bytes=16 * 2**20),
        cost_estimate=pl.CostEstimate(flops=0, bytes_accessed=2**20, transcendentals=0),
    )(ids, keep, got)


def pin(values):
    return lax.optimization_barrier(values)


def turn(size, shift):
    return [(i, (i + shift) % size) for i in range(size)]


def shards(inverse_root, panel, block_mask, diag_inverse):
    ix, iz, ic = lax.axis_index("x"), lax.axis_index("zh"), lax.axis_index("core")
    col = lax.axis_index("zl") * 4 + lax.axis_index("y")
    ids = jnp.stack([ix, iz, ic, col]).astype(jnp.int32)
    swap = [(0, 1), (1, 0)]

    def sum_parts(parts):
        return jnp.sum(parts.astype(jnp.float32), axis=0) * (1.0 / SCALE)

    def send_parts(partial):
        return partial.astype(jnp.float16)

    def around(slab):
        return [lax.ppermute(slab, "x", turn(4, 1)), lax.ppermute(slab, "x", turn(4, -1))]

    def to_columns(value):
        return lax.all_to_all(value, ("zl", "y"), 0, 0, tiled=True)

    def to_rows(value):
        return lax.all_to_all(value, ("x", "zh"), 0, 0, tiled=True)

    other_root = lax.ppermute(inverse_root, "core", swap)
    own, pieces = mask_call(ids, block_mask, jnp.transpose(panel, (1, 2, 0)).reshape(64, 2048))

    z1, z3 = (lax.ppermute(own, "zh", turn(4, s)) for s in (1, 3))
    near0, pieces = pin((around(own), pieces))
    far0 = lax.ppermute(near0[0], "x", turn(4, 1))
    pieces = to_columns(pieces)
    z1, z3, near0, far0, own, other_root = pin((z1, z3, near0, far0, own, other_root))

    z2 = lax.ppermute(own, "zh", turn(4, 2))
    near1, near3 = around(z1), around(z3)
    mine = to_rows(hold_call(mark_call(own), pieces.reshape(16, 64, 128)))
    z2, near1, near3 = pin((z2, near1, near3))

    far1, far3 = lax.ppermute(near1[0], "x", turn(4, 1)), lax.ppermute(near3[1], "x", turn(4, -1))
    near2 = around(z2)
    early = send_parts(product_call(ids, [own, *near0, far0, z1, *near1, z3, *near3], inverse_root, other_root, 58))
    far1, far3, near2, early, mine = pin((far1, far3, near2, early, mine))

    parts = to_columns(early)
    far2 = lax.ppermute(near2[0], "x", turn(4, 1))
    far2 = pin((far2,))[0]

    late = send_parts(product_call(ids, [far1, far3, z2, *near2, far2], inverse_root, other_root, 24))
    late, parts = pin((late, parts))
    other = lax.ppermute(mine, "core", swap)
    keep, give, diag = diag_call(ids, sum_parts(parts), sum_parts(to_columns(late)), mine, other)
    got = lax.ppermute(give, "core", swap)
    here = jnp.sum(to_columns(diag.astype(jnp.float16)).astype(jnp.float32), axis=0)
    panel_inverse = rows_call(ids, keep, got)
    here, panel_inverse = lax.optimization_barrier((here, panel_inverse))
    across = here.reshape(128, 256).T.reshape(2, 16, 8, 128)
    across = jnp.transpose(across, (1, 0, 2, 3))
    here = jnp.sum(to_rows(across), axis=0)
    came = lax.ppermute(here[1], "core", swap)
    even, odd = jnp.where(ic == 0, here[0], came), jnp.where(ic == 0, came, here[0])
    both = jnp.stack([even.reshape(8, 8, 2, 8), odd.reshape(8, 8, 2, 8)], axis=3)
    block = jnp.transpose(both, (1, 0, 2, 3, 4)).reshape(8, 8, 32)
    return panel_inverse, diag_inverse + block


def solution(mesh):
    wide = Mesh(mesh.devices.reshape(4, 4, 2, 2, 4), ("x", "zh", "core", "zl", "y"))
    prow, pcol = ("x", "zh", "core"), ("zl", "y")
    in_specs = (P(prow, pcol), P(pcol, None, prow), P(), P(None, prow, pcol))
    out_specs = (P(prow + pcol, None, None), P(None, prow, pcol))
    return jax.shard_map(shards, mesh=wide, in_specs=in_specs, out_specs=out_specs, check_vma=False)
```

```python
import functools

import jax
import jax.numpy as jnp
from jax import lax
from jax.experimental import pallas as pl
from jax.experimental.pallas import tpu as pltpu
from jax.sharding import Mesh, PartitionSpec as P

EARLY = ((0, 0), (3, 0), (1, 0), (2, 0), (0, 1), (3, 1), (1, 1), (0, 3), (3, 3), (1, 3))
LATE = ((2, 1), (2, 3), (0, 2), (3, 2), (1, 2), (2, 2))
SCALE = 64.0
NT = (((1,), (1,)), ((), ()))
VMEM = pl.BlockSpec(memory_space=pltpu.VMEM)
ANY = pl.BlockSpec(memory_space=pl.ANY)
SMEM = pl.BlockSpec(memory_space=pltpu.SMEM)


def mask_kernel(ids, mask, panel, own, pieces):
    ic, col, t = ids[2], ids[3], pl.program_id(0)
    upper = lax.broadcasted_iota(jnp.int32, (16, 256), 0) < 8
    low = lax.broadcasted_iota(jnp.int32, (16, 128), 1) < 64
    blocks = []
    for i in range(8):
        lanes = slice(256 * i, 256 * i + 256)
        here = jnp.where(upper, mask[2 * t, col * 8 + i], mask[2 * t + 1, col * 8 + i]).astype(jnp.float32)
        blocks.append(panel[:, lanes].astype(jnp.float32) * here)
        own[:, lanes] = blocks[-1].astype(own.dtype)
    for b in range(2):
        for h in range(2):
            even, odd = blocks[4 * b + h], blocks[4 * b + 2 + h]
            first, second = jnp.where(ic == 0, even, odd), jnp.where(ic == 0, odd, even)
            for u in range(2):
                p, q = first[:, 128 * u:128 * u + 128], second[:, 128 * u:128 * u + 128]
                j = 4 * h + 2 * u
                pieces[j, b] = jnp.where(low, p, pltpu.roll(q, 64, 1)).astype(pieces.dtype)
                pieces[j + 1, b] = jnp.where(low, pltpu.roll(p, 64, 1), q).astype(pieces.dtype)


def mask_call(ids, mask, panel):
    return pl.pallas_call(
        mask_kernel,
        grid=(4,),
        out_shape=(
            jax.ShapeDtypeStruct((64, 2048), jnp.bfloat16),
            jax.ShapeDtypeStruct((8, 2, 64, 128), jnp.bfloat16),
        ),
        in_specs=[SMEM, SMEM, pl.BlockSpec((16, 2048), lambda t: (t, 0))],
        out_specs=(
            pl.BlockSpec((16, 2048), lambda t: (t, 0)),
            pl.BlockSpec((8, 2, 16, 128), lambda t: (0, 0, t, 0)),
        ),
        compiler_params=pltpu.CompilerParams(vmem_limit_bytes=60 * 2**20),
        cost_estimate=pl.CostEstimate(flops=1, bytes_accessed=2**20, transcendentals=0),
    )(ids, mask, panel)


def product_kernel(ids, *refs):
    slabs, (root, other_root, out, gathered, pair) = refs[:-5], refs[-5:]

    @pl.when(pl.program_id(0) == 0)
    def _():
        start = 0
        for slab in slabs:
            gathered[start:start + slab.shape[0], :] = slab[...]
            start += slab.shape[0]

    for j in range(2):
        pair[128 * j:128 * j + 64, :] = root[64 * j:64 * j + 64, :]
        pair[128 * j + 64:128 * j + 128, :] = other_root[64 * j:64 * j + 64, :]
    prod = lax.dot_general(gathered[...], pair[...], NT, preferred_element_type=jnp.float32)
    out[0] = prod[:, 0:128] * SCALE
    out[1] = prod[:, 128:256] * SCALE


def product_call(ids, slabs, root, other_root, vmem):
    n = sum(slab.shape[0] for slab in slabs)
    return pl.pallas_call(
        product_kernel,
        grid=(4,),
        out_shape=jax.ShapeDtypeStruct((8, n, 128), jnp.float32),
        in_specs=[SMEM] + [pl.BlockSpec(slab.shape, lambda t: (0, 0)) for slab in slabs]
        + [pl.BlockSpec((128, 2048), lambda t: (t, 0))] * 2,
        out_specs=pl.BlockSpec((2, n, 128), lambda t: (t, 0, 0)),
        scratch_shapes=[pltpu.VMEM((n, 2048), jnp.bfloat16), pltpu.VMEM((256, 2048), jnp.bfloat16)],
        compiler_params=pltpu.CompilerParams(vmem_limit_bytes=vmem * 2**20),
        cost_estimate=pl.CostEstimate(flops=2 * n * 2048 * 1024, bytes_accessed=2 * n * 2048 + 6 * 2**20, transcendentals=0),
    )(ids, *slabs, root, other_root)


def mark_kernel(source, out):
    out[...] = jnp.zeros_like(out)


def mark_call(value):
    return pl.pallas_call(
        mark_kernel,
        out_shape=jax.ShapeDtypeStruct((8, 128), jnp.float32),
        in_specs=[ANY],
        out_specs=VMEM,
        cost_estimate=pl.CostEstimate(flops=2**34, bytes_accessed=2**12, transcendentals=0),
    )(value)


def hold_kernel(after, source, out):
    pass


def hold_call(after, value):
    return pl.pallas_call(
        hold_kernel,
        out_shape=jax.ShapeDtypeStruct(value.shape, value.dtype),
        in_specs=[ANY, ANY],
        out_specs=ANY,
        input_output_aliases={1: 0},
        cost_estimate=pl.CostEstimate(flops=2**34, bytes_accessed=2**12, transcendentals=0),
    )(after, value)


def diag_kernel(ids, early, late, mine, other, keep, give, diag):
    ix, iz = ids[0], ids[1]
    low = lax.broadcasted_iota(jnp.int32, (8, 128), 1) < 64
    left = mine[...].astype(jnp.float32).reshape(16, 8, 8, 128)
    right = pltpu.roll(other[...].astype(jnp.float32), 64, 2).reshape(16, 8, 8, 128)
    totals, places = [], []
    slabs = [early[64 * i:64 * i + 64, :] for i in range(len(EARLY))] + [late[64 * i:64 * i + 64, :] for i in range(len(LATE))]
    for slab, (dx, dz) in zip(slabs, EARLY + LATE):
        total = slab.reshape(8, 8, 128)
        x, z = lax.rem(ix + dx, 4), lax.rem(iz + 4 - dz, 4)
        totals.append(total)
        places.append((2 * x + lax.div(z, 2), lax.rem(z, 2)))
        for t in range(4):
            even, odd = total[2 * t], total[2 * t + 1]
            keep[t, x, z] = -jnp.where(low, even, pltpu.roll(odd, 64, 1))
            give[t, x, z] = -jnp.where(low, pltpu.roll(even, 64, 1), odd)
    for k in range(8):
        p = jnp.concatenate([total[k] for total in totals], axis=0)
        hi = p.astype(jnp.bfloat16)
        rest = p - hi.astype(jnp.float32)
        mid = rest.astype(jnp.bfloat16)
        lo = (rest - mid.astype(jnp.float32)).astype(jnp.bfloat16)
        m = jnp.concatenate([left[:, k].reshape(128, 128), right[:, k].reshape(128, 128)], axis=0).astype(jnp.bfloat16)
        d = lax.dot_general(lo, m, NT, preferred_element_type=jnp.float32)
        d += lax.dot_general(mid, m, NT, preferred_element_type=jnp.float32)
        d += lax.dot_general(hi, m, NT, preferred_element_type=jnp.float32)
        for i, (column, z) in enumerate(places):
            diag[column, k, z] = d[i * 8:(i + 1) * 8, :]


def diag_call(ids, early, late, mine, other):
    return pl.pallas_call(
        diag_kernel,
        out_shape=(
            jax.ShapeDtypeStruct((4, 4, 4, 8, 128), jnp.float32),
            jax.ShapeDtypeStruct((4, 4, 4, 8, 128), jnp.float32),
            jax.ShapeDtypeStruct((8, 8, 2, 8, 256), jnp.float32),
        ),
        in_specs=[SMEM] + [VMEM] * 4,
        out_specs=(VMEM,) * 3,
        compiler_params=pltpu.CompilerParams(vmem_limit_bytes=16 * 2**20),
        cost_estimate=pl.CostEstimate(flops=2 * 8 * 3 * 128 * 128 * 256, bytes_accessed=2**23, transcendentals=0),
    )(ids, early, late, mine, other)


def rows_kernel(ids, keep, got, out):
    first = ids[2] == 0
    for t in range(4):
        a, b = keep[t].reshape(16, 1, 8, 128), got[t].reshape(16, 1, 8, 128)
        even, odd = jnp.where(first, a, b), jnp.where(first, b, a)
        both = jnp.concatenate([even, odd], axis=1).reshape(256, 128).T
        out[:, 2 * t, :] = both[0:64, :]
        out[:, 2 * t + 1, :] = both[64:128, :]


def rows_call(ids, keep, got):
    return pl.pallas_call(
        rows_kernel,
        out_shape=jax.ShapeDtypeStruct((64, 8, 256), jnp.float32),
        in_specs=[SMEM, VMEM, VMEM],
        out_specs=VMEM,
        compiler_params=pltpu.CompilerParams(vmem_limit_bytes=16 * 2**20),
        cost_estimate=pl.CostEstimate(flops=0, bytes_accessed=2**20, transcendentals=0),
    )(ids, keep, got)


def pin(values):
    return lax.optimization_barrier(values)


def turn(size, shift):
    return [(i, (i + shift) % size) for i in range(size)]


def shards(inverse_root, panel, block_mask, diag_inverse):
    ix, iz, ic = lax.axis_index("x"), lax.axis_index("zh"), lax.axis_index("core")
    col = lax.axis_index("zl") * 4 + lax.axis_index("y")
    ids = jnp.stack([ix, iz, ic, col]).astype(jnp.int32)
    swap = [(0, 1), (1, 0)]

    def sum_parts(parts):
        return jnp.sum(parts.astype(jnp.float32), axis=0) * (1.0 / SCALE)

    def send_parts(partial):
        return partial.astype(jnp.float16)

    def around(slab):
        return [lax.ppermute(slab, "x", turn(4, 1)), lax.ppermute(slab, "x", turn(4, -1))]

    def to_columns(value):
        return lax.all_to_all(value, ("zl", "y"), 0, 0, tiled=True)

    def to_rows(value):
        return lax.all_to_all(value, ("x", "zh"), 0, 0, tiled=True)

    other_root = lax.ppermute(inverse_root, "core", swap)
    own, pieces = mask_call(ids, block_mask, jnp.transpose(panel, (1, 2, 0)).reshape(64, 2048))

    z1, z3 = (lax.ppermute(own, "zh", turn(4, s)) for s in (1, 3))
    near0, pieces = pin((around(own), pieces))
    far0 = lax.ppermute(near0[0], "x", turn(4, 1))
    pieces = to_columns(pieces)
    z1, z3, near0, far0, own, other_root = pin((z1, z3, near0, far0, own, other_root))

    z2 = lax.ppermute(z1, "zh", turn(4, 1))
    near1, near3 = around(z1), around(z3)
    mine = to_rows(hold_call(mark_call(own), pieces.reshape(16, 64, 128)))
    z2, near1, near3 = pin((z2, near1, near3))

    far1, far3 = lax.ppermute(near1[0], "x", turn(4, 1)), lax.ppermute(near3[1], "x", turn(4, -1))
    near2 = around(z2)
    early = send_parts(product_call(ids, [own, *near0, far0, z1, *near1, z3, *near3], inverse_root, other_root, 58))
    far1, far3, near2, early, mine = pin((far1, far3, near2, early, mine))

    parts = to_columns(early)
    far2 = lax.ppermute(near2[0], "x", turn(4, 1))
    far2 = pin((far2,))[0]

    late = send_parts(product_call(ids, [far1, far3, z2, *near2, far2], inverse_root, other_root, 24))
    late, parts = pin((late, parts))
    other = lax.ppermute(mine, "core", swap)
    keep, give, diag = diag_call(ids, sum_parts(parts), sum_parts(to_columns(late)), mine, other)
    got = lax.ppermute(give, "core", swap)
    here = jnp.sum(to_columns(diag.astype(jnp.float16)).astype(jnp.float32), axis=0)
    panel_inverse = rows_call(ids, keep, got)
    here, panel_inverse = lax.optimization_barrier((here, panel_inverse))
    across = here.reshape(128, 256).T.reshape(2, 16, 8, 128)
    across = jnp.transpose(across, (1, 0, 2, 3))
    here = jnp.sum(to_rows(across), axis=0)
    came = lax.ppermute(here[1], "core", swap)
    even, odd = jnp.where(ic == 0, here[0], came), jnp.where(ic == 0, came, here[0])
    both = jnp.stack([even.reshape(8, 8, 2, 8), odd.reshape(8, 8, 2, 8)], axis=3)
    block = jnp.transpose(both, (1, 0, 2, 3, 4)).reshape(8, 8, 32)
    return panel_inverse, diag_inverse + block


def solution(mesh):
    wide = Mesh(mesh.devices.reshape(4, 4, 2, 2, 4), ("x", "zh", "core", "zl", "y"))
    prow, pcol = ("x", "zh", "core"), ("zl", "y")
    in_specs = (P(prow, pcol), P(pcol, None, prow), P(), P(None, prow, pcol))
    out_specs = (P(prow + pcol, None, None), P(None, prow, pcol))
    return jax.shard_map(shards, mesh=wide, in_specs=in_specs, out_specs=out_specs, check_vma=False)
```

```python
import functools

import jax
import jax.numpy as jnp
from jax import lax
from jax.experimental import pallas as pl
from jax.experimental.pallas import tpu as pltpu
from jax.sharding import Mesh, PartitionSpec as P

EARLY = ((0, 0), (3, 0), (1, 0), (2, 0), (0, 1), (3, 1), (1, 1), (0, 3), (3, 3), (1, 3))
LATE = ((2, 1), (2, 3), (0, 2), (3, 2), (1, 2), (2, 2))
SCALE = 64.0
NT = (((1,), (1,)), ((), ()))
VMEM = pl.BlockSpec(memory_space=pltpu.VMEM)
ANY = pl.BlockSpec(memory_space=pl.ANY)
SMEM = pl.BlockSpec(memory_space=pltpu.SMEM)


def mask_kernel(mask, panel, own):
    col = lax.axis_index("zl") * 4 + lax.axis_index("y")
    upper = lax.broadcasted_iota(jnp.int32, (16, 256), 0) < 8
    for t in range(4):
        rows = slice(16 * t, 16 * t + 16)
        for i in range(8):
            lanes = slice(256 * i, 256 * i + 256)
            here = jnp.where(upper, mask[2 * t, col * 8 + i], mask[2 * t + 1, col * 8 + i]).astype(jnp.float32)
            own[rows, lanes] = (panel[rows, lanes].astype(jnp.float32) * here).astype(own.dtype)


def mask_call(mask, panel):
    return pl.pallas_call(
        mask_kernel,
        out_shape=jax.ShapeDtypeStruct((64, 2048), jnp.bfloat16),
        in_specs=[SMEM, VMEM],
        out_specs=VMEM,
        cost_estimate=pl.CostEstimate(flops=1, bytes_accessed=2**19, transcendentals=0),
    )(mask, panel)


def pieces_kernel(ids, own, pieces):
    ic = ids[2]
    low = lax.broadcasted_iota(jnp.int32, (64, 128), 1) < 64
    for b in range(2):
        for u in range(4):
            lanes = [slice(1024 * b + 512 * c + 128 * u, 1024 * b + 512 * c + 128 * u + 128) for c in range(2)]
            even, odd = own[:, lanes[0]].astype(jnp.float32), own[:, lanes[1]].astype(jnp.float32)
            p, q = jnp.where(ic == 0, even, odd), jnp.where(ic == 0, odd, even)
            pieces[2 * u, b] = jnp.where(low, p, pltpu.roll(q, 64, 1)).astype(pieces.dtype)
            pieces[2 * u + 1, b] = jnp.where(low, pltpu.roll(p, 64, 1), q).astype(pieces.dtype)


def pieces_call(ids, own):
    return pl.pallas_call(
        pieces_kernel,
        out_shape=jax.ShapeDtypeStruct((8, 2, 64, 128), jnp.bfloat16),
        in_specs=[SMEM, VMEM],
        out_specs=VMEM,
        cost_estimate=pl.CostEstimate(flops=1, bytes_accessed=2**19, transcendentals=0),
    )(ids, own)


def product_kernel(ids, *refs):
    slabs, (root, other_root, out, gathered, pair) = refs[:-5], refs[-5:]

    @pl.when(pl.program_id(0) == 0)
    def _():
        start = 0
        for slab in slabs:
            gathered[start:start + slab.shape[0], :] = slab[...]
            start += slab.shape[0]

    for j in range(2):
        pair[128 * j:128 * j + 64, :] = root[64 * j:64 * j + 64, :]
        pair[128 * j + 64:128 * j + 128, :] = other_root[64 * j:64 * j + 64, :]
    prod = lax.dot_general(gathered[...], pair[...], NT, preferred_element_type=jnp.float32)
    out[0] = prod[:, 0:128] * SCALE
    out[1] = prod[:, 128:256] * SCALE


def product_call(ids, slabs, root, other_root, vmem):
    n = sum(slab.shape[0] for slab in slabs)
    return pl.pallas_call(
        product_kernel,
        grid=(4,),
        out_shape=jax.ShapeDtypeStruct((8, n, 128), jnp.float32),
        in_specs=[SMEM] + [pl.BlockSpec(slab.shape, lambda t: (0, 0)) for slab in slabs]
        + [pl.BlockSpec((128, 2048), lambda t: (t, 0))] * 2,
        out_specs=pl.BlockSpec((2, n, 128), lambda t: (t, 0, 0)),
        scratch_shapes=[pltpu.VMEM((n, 2048), jnp.bfloat16), pltpu.VMEM((256, 2048), jnp.bfloat16)],
        compiler_params=pltpu.CompilerParams(vmem_limit_bytes=vmem * 2**20),
        cost_estimate=pl.CostEstimate(flops=2 * n * 2048 * 1024, bytes_accessed=2 * n * 2048 + 6 * 2**20, transcendentals=0),
    )(ids, *slabs, root, other_root)


def mark_kernel(source, out):
    out[...] = jnp.zeros_like(out)


def mark_call(value):
    return pl.pallas_call(
        mark_kernel,
        out_shape=jax.ShapeDtypeStruct((8, 128), jnp.float32),
        in_specs=[ANY],
        out_specs=VMEM,
        cost_estimate=pl.CostEstimate(flops=2**34, bytes_accessed=2**12, transcendentals=0),
    )(value)


def hold_kernel(after, source, out):
    pass


def hold_call(after, value):
    return pl.pallas_call(
        hold_kernel,
        out_shape=jax.ShapeDtypeStruct(value.shape, value.dtype),
        in_specs=[ANY, ANY],
        out_specs=ANY,
        input_output_aliases={1: 0},
        cost_estimate=pl.CostEstimate(flops=2**34, bytes_accessed=2**12, transcendentals=0),
    )(after, value)


def diag_kernel(ids, early, late, mine, other, keep, give, diag):
    ix, iz = ids[0], ids[1]
    low = lax.broadcasted_iota(jnp.int32, (8, 128), 1) < 64
    left = mine[...].astype(jnp.float32).reshape(16, 8, 8, 128)
    right = pltpu.roll(other[...].astype(jnp.float32), 64, 2).reshape(16, 8, 8, 128)
    totals, places = [], []
    slabs = [early[64 * i:64 * i + 64, :] for i in range(len(EARLY))] + [late[64 * i:64 * i + 64, :] for i in range(len(LATE))]
    for slab, (dx, dz) in zip(slabs, EARLY + LATE):
        total = slab.reshape(8, 8, 128)
        x, z = lax.rem(ix + dx, 4), lax.rem(iz + 4 - dz, 4)
        totals.append(total)
        places.append((2 * x + lax.div(z, 2), lax.rem(z, 2)))
        for t in range(4):
            even, odd = total[2 * t], total[2 * t + 1]
            keep[t, x, z] = -jnp.where(low, even, pltpu.roll(odd, 64, 1))
            give[t, x, z] = -jnp.where(low, pltpu.roll(even, 64, 1), odd)
    for k in range(8):
        p = jnp.concatenate([total[k] for total in totals], axis=0)
        hi = p.astype(jnp.bfloat16)
        rest = p - hi.astype(jnp.float32)
        mid = rest.astype(jnp.bfloat16)
        lo = (rest - mid.astype(jnp.float32)).astype(jnp.bfloat16)
        m = jnp.concatenate([left[:, k].reshape(128, 128), right[:, k].reshape(128, 128)], axis=0).astype(jnp.bfloat16)
        d = lax.dot_general(lo, m, NT, preferred_element_type=jnp.float32)
        d += lax.dot_general(mid, m, NT, preferred_element_type=jnp.float32)
        d += lax.dot_general(hi, m, NT, preferred_element_type=jnp.float32)
        for i, (column, z) in enumerate(places):
            diag[column, k, z] = d[i * 8:(i + 1) * 8, :]


def diag_call(ids, early, late, mine, other):
    return pl.pallas_call(
        diag_kernel,
        out_shape=(
            jax.ShapeDtypeStruct((4, 4, 4, 8, 128), jnp.float32),
            jax.ShapeDtypeStruct((4, 4, 4, 8, 128), jnp.float32),
            jax.ShapeDtypeStruct((8, 8, 2, 8, 256), jnp.float32),
        ),
        in_specs=[SMEM] + [VMEM] * 4,
        out_specs=(VMEM,) * 3,
        compiler_params=pltpu.CompilerParams(vmem_limit_bytes=16 * 2**20),
        cost_estimate=pl.CostEstimate(flops=2 * 8 * 3 * 128 * 128 * 256, bytes_accessed=2**23, transcendentals=0),
    )(ids, early, late, mine, other)


def rows_kernel(ids, keep, got, out):
    first = ids[2] == 0
    for t in range(4):
        a, b = keep[t].reshape(16, 1, 8, 128), got[t].reshape(16, 1, 8, 128)
        even, odd = jnp.where(first, a, b), jnp.where(first, b, a)
        both = jnp.concatenate([even, odd], axis=1).reshape(256, 128).T
        out[:, 2 * t, :] = both[0:64, :]
        out[:, 2 * t + 1, :] = both[64:128, :]


def rows_call(ids, keep, got):
    return pl.pallas_call(
        rows_kernel,
        out_shape=jax.ShapeDtypeStruct((64, 8, 256), jnp.float32),
        in_specs=[SMEM, VMEM, VMEM],
        out_specs=VMEM,
        compiler_params=pltpu.CompilerParams(vmem_limit_bytes=16 * 2**20),
        cost_estimate=pl.CostEstimate(flops=0, bytes_accessed=2**20, transcendentals=0),
    )(ids, keep, got)


def pin(values):
    return lax.optimization_barrier(values)


def turn(size, shift):
    return [(i, (i + shift) % size) for i in range(size)]


def shards(inverse_root, panel, block_mask, diag_inverse):
    ix, iz, ic = lax.axis_index("x"), lax.axis_index("zh"), lax.axis_index("core")
    col = lax.axis_index("zl") * 4 + lax.axis_index("y")
    ids = jnp.stack([ix, iz, ic, col]).astype(jnp.int32)
    swap = [(0, 1), (1, 0)]

    def sum_parts(parts):
        return jnp.sum(parts.astype(jnp.float32), axis=0) * (1.0 / SCALE)

    def send_parts(partial):
        return partial.astype(jnp.float16)

    def around(slab):
        return [lax.ppermute(slab, "x", turn(4, 1)), lax.ppermute(slab, "x", turn(4, -1))]

    def to_columns(value):
        return lax.all_to_all(value, ("zl", "y"), 0, 0, tiled=True)

    def to_rows(value):
        return lax.all_to_all(value, ("x", "zh"), 0, 0, tiled=True)

    other_root = lax.ppermute(inverse_root, "core", swap)
    own = mask_call(block_mask, jnp.transpose(panel, (1, 2, 0)).reshape(64, 2048))
    pieces = pieces_call(ids, own)

    z1, z3 = (lax.ppermute(own, "zh", turn(4, s)) for s in (1, 3))
    near0, pieces = pin((around(own), pieces))
    far0 = lax.ppermute(near0[0], "x", turn(4, 1))
    pieces = to_columns(pieces)
    z1, z3, near0, far0, own, other_root = pin((z1, z3, near0, far0, own, other_root))

    z2 = lax.ppermute(z1, "zh", turn(4, 1))
    near1, near3 = around(z1), around(z3)
    mine = to_rows(hold_call(mark_call(own), pieces.reshape(16, 64, 128)))
    z2, near1, near3 = pin((z2, near1, near3))

    far1, far3 = lax.ppermute(near1[0], "x", turn(4, 1)), lax.ppermute(near3[1], "x", turn(4, -1))
    near2 = around(z2)
    early = send_parts(product_call(ids, [own, *near0, far0, z1, *near1, z3, *near3], inverse_root, other_root, 58))
    far1, far3, near2, early, mine = pin((far1, far3, near2, early, mine))

    parts = to_columns(early)
    far2 = lax.ppermute(near2[0], "x", turn(4, 1))
    far2 = pin((far2,))[0]

    late = send_parts(product_call(ids, [far1, far3, z2, *near2, far2], inverse_root, other_root, 24))
    late, parts = pin((late, parts))
    other = lax.ppermute(mine, "core", swap)
    keep, give, diag = diag_call(ids, sum_parts(parts), sum_parts(to_columns(late)), mine, other)
    got = lax.ppermute(give, "core", swap)
    here = jnp.sum(to_columns(diag.astype(jnp.float16)).astype(jnp.float32), axis=0)
    panel_inverse = rows_call(ids, keep, got)
    here, panel_inverse = lax.optimization_barrier((here, panel_inverse))
    across = here.reshape(128, 256).T.reshape(2, 16, 8, 128)
    across = jnp.transpose(across, (1, 0, 2, 3))
    here = jnp.sum(to_rows(across), axis=0)
    came = lax.ppermute(here[1], "core", swap)
    even, odd = jnp.where(ic == 0, here[0], came), jnp.where(ic == 0, came, here[0])
    both = jnp.stack([even.reshape(8, 8, 2, 8), odd.reshape(8, 8, 2, 8)], axis=3)
    block = jnp.transpose(both, (1, 0, 2, 3, 4)).reshape(8, 8, 32)
    return panel_inverse, diag_inverse + block


def solution(mesh):
    wide = Mesh(mesh.devices.reshape(4, 4, 2, 2, 4), ("x", "zh", "core", "zl", "y"))
    prow, pcol = ("x", "zh", "core"), ("zl", "y")
    in_specs = (P(prow, pcol), P(pcol, None, prow), P(), P(None, prow, pcol))
    out_specs = (P(prow + pcol, None, None), P(None, prow, pcol))
    return jax.shard_map(shards, mesh=wide, in_specs=in_specs, out_specs=out_specs, check_vma=False)
```

```python
import functools

import jax
import jax.numpy as jnp
from jax import lax
from jax.experimental import pallas as pl
from jax.experimental.pallas import tpu as pltpu
from jax.sharding import Mesh, PartitionSpec as P

EARLY = ((0, 0), (3, 0), (1, 0), (2, 0), (0, 1), (3, 1), (1, 1), (0, 3))
LATE = ((3, 3), (1, 3), (2, 1), (2, 3), (0, 2), (3, 2), (1, 2), (2, 2))
SCALE = 64.0
NT = (((1,), (1,)), ((), ()))
VMEM = pl.BlockSpec(memory_space=pltpu.VMEM)
ANY = pl.BlockSpec(memory_space=pl.ANY)
SMEM = pl.BlockSpec(memory_space=pltpu.SMEM)


def mask_kernel(mask, panel, own):
    col = lax.axis_index("zl") * 4 + lax.axis_index("y")
    upper = lax.broadcasted_iota(jnp.int32, (16, 256), 0) < 8
    for t in range(4):
        rows = slice(16 * t, 16 * t + 16)
        for i in range(8):
            lanes = slice(256 * i, 256 * i + 256)
            here = jnp.where(upper, mask[2 * t, col * 8 + i], mask[2 * t + 1, col * 8 + i]).astype(jnp.float32)
            own[rows, lanes] = (panel[rows, lanes].astype(jnp.float32) * here).astype(own.dtype)


def mask_call(mask, panel):
    return pl.pallas_call(
        mask_kernel,
        out_shape=jax.ShapeDtypeStruct((64, 2048), jnp.bfloat16),
        in_specs=[SMEM, VMEM],
        out_specs=VMEM,
        cost_estimate=pl.CostEstimate(flops=1, bytes_accessed=2**19, transcendentals=0),
    )(mask, panel)


def pieces_kernel(own, pieces):
    ic = lax.axis_index("core")
    low = lax.broadcasted_iota(jnp.int32, (64, 128), 1) < 64
    for b in range(2):
        for u in range(4):
            lanes = [slice(1024 * b + 512 * c + 128 * u, 1024 * b + 512 * c + 128 * u + 128) for c in range(2)]
            even, odd = own[:, lanes[0]].astype(jnp.float32), own[:, lanes[1]].astype(jnp.float32)
            p, q = jnp.where(ic == 0, even, odd), jnp.where(ic == 0, odd, even)
            pieces[2 * u, b] = jnp.where(low, p, pltpu.roll(q, 64, 1)).astype(pieces.dtype)
            pieces[2 * u + 1, b] = jnp.where(low, pltpu.roll(p, 64, 1), q).astype(pieces.dtype)


def pieces_call(own):
    return pl.pallas_call(
        pieces_kernel,
        out_shape=jax.ShapeDtypeStruct((8, 2, 64, 128), jnp.bfloat16),
        in_specs=[VMEM],
        out_specs=VMEM,
        cost_estimate=pl.CostEstimate(flops=1, bytes_accessed=2**19, transcendentals=0),
    )(own)


def product_kernel(*refs):
    slabs, (root, other_root, out, gathered, pair) = refs[:-5], refs[-5:]

    @pl.when(pl.program_id(0) == 0)
    def _():
        start = 0
        for slab in slabs:
            gathered[start:start + slab.shape[0], :] = slab[...]
            start += slab.shape[0]

    for j in range(2):
        pair[128 * j:128 * j + 64, :] = root[64 * j:64 * j + 64, :]
        pair[128 * j + 64:128 * j + 128, :] = other_root[64 * j:64 * j + 64, :]
    prod = lax.dot_general(gathered[...], pair[...], NT, preferred_element_type=jnp.float32)
    out[0] = prod[:, 0:128] * SCALE
    out[1] = prod[:, 128:256] * SCALE


def product_call(slabs, root, other_root, vmem):
    n = sum(slab.shape[0] for slab in slabs)
    return pl.pallas_call(
        product_kernel,
        grid=(4,),
        out_shape=jax.ShapeDtypeStruct((8, n, 128), jnp.float32),
        in_specs=[pl.BlockSpec(slab.shape, lambda t: (0, 0)) for slab in slabs]
        + [pl.BlockSpec((128, 2048), lambda t: (t, 0))] * 2,
        out_specs=pl.BlockSpec((2, n, 128), lambda t: (t, 0, 0)),
        scratch_shapes=[pltpu.VMEM((n, 2048), jnp.bfloat16), pltpu.VMEM((256, 2048), jnp.bfloat16)],
        compiler_params=pltpu.CompilerParams(vmem_limit_bytes=vmem * 2**20),
        cost_estimate=pl.CostEstimate(flops=2 * n * 2048 * 1024, bytes_accessed=2 * n * 2048 + 6 * 2**20, transcendentals=0),
    )(*slabs, root, other_root)


def mark_kernel(source, out):
    out[...] = jnp.zeros_like(out)


def mark_call(value):
    return pl.pallas_call(
        mark_kernel,
        out_shape=jax.ShapeDtypeStruct((8, 128), jnp.float32),
        in_specs=[ANY],
        out_specs=VMEM,
        cost_estimate=pl.CostEstimate(flops=2**34, bytes_accessed=2**12, transcendentals=0),
    )(value)


def hold_kernel(after, source, out):
    pass


def hold_call(after, value):
    return pl.pallas_call(
        hold_kernel,
        out_shape=jax.ShapeDtypeStruct(value.shape, value.dtype),
        in_specs=[ANY, ANY],
        out_specs=ANY,
        input_output_aliases={1: 0},
        cost_estimate=pl.CostEstimate(flops=2**34, bytes_accessed=2**12, transcendentals=0),
    )(after, value)


def diag_kernel(early, late, mine, other, keep, give, diag):
    ix, iz = lax.axis_index("x"), lax.axis_index("zh")
    low = lax.broadcasted_iota(jnp.int32, (8, 128), 1) < 64
    left = mine[...].astype(jnp.float32).reshape(16, 8, 8, 128)
    right = pltpu.roll(other[...].astype(jnp.float32), 64, 2).reshape(16, 8, 8, 128)
    totals, places = [], []
    slabs = [early[64 * i:64 * i + 64, :] for i in range(len(EARLY))] + [late[64 * i:64 * i + 64, :] for i in range(len(LATE))]
    for slab, (dx, dz) in zip(slabs, EARLY + LATE):
        total = slab.reshape(8, 8, 128)
        x, z = lax.rem(ix + dx, 4), lax.rem(iz + 4 - dz, 4)
        totals.append(total)
        places.append((2 * x + lax.div(z, 2), lax.rem(z, 2)))
        for t in range(4):
            even, odd = total[2 * t], total[2 * t + 1]
            keep[t, x, z] = -jnp.where(low, even, pltpu.roll(odd, 64, 1))
            give[t, x, z] = -jnp.where(low, pltpu.roll(even, 64, 1), odd)
    for k in range(8):
        p = jnp.concatenate([total[k] for total in totals], axis=0)
        hi = p.astype(jnp.bfloat16)
        rest = p - hi.astype(jnp.float32)
        mid = rest.astype(jnp.bfloat16)
        lo = (rest - mid.astype(jnp.float32)).astype(jnp.bfloat16)
        m = jnp.concatenate([left[:, k].reshape(128, 128), right[:, k].reshape(128, 128)], axis=0).astype(jnp.bfloat16)
        d = lax.dot_general(lo, m, NT, preferred_element_type=jnp.float32)
        d += lax.dot_general(mid, m, NT, preferred_element_type=jnp.float32)
        d += lax.dot_general(hi, m, NT, preferred_element_type=jnp.float32)
        for i, (column, z) in enumerate(places):
            diag[column, k, z] = d[i * 8:(i + 1) * 8, :]


def diag_call(early, late, mine, other):
    return pl.pallas_call(
        diag_kernel,
        out_shape=(
            jax.ShapeDtypeStruct((4, 4, 4, 8, 128), jnp.float32),
            jax.ShapeDtypeStruct((4, 4, 4, 8, 128), jnp.float32),
            jax.ShapeDtypeStruct((8, 8, 2, 8, 256), jnp.float32),
        ),
        in_specs=[VMEM] * 4,
        out_specs=(VMEM,) * 3,
        compiler_params=pltpu.CompilerParams(vmem_limit_bytes=16 * 2**20),
        cost_estimate=pl.CostEstimate(flops=2 * 8 * 3 * 128 * 128 * 256, bytes_accessed=2**23, transcendentals=0),
    )(early, late, mine, other)


def rows_kernel(keep, got, out):
    first = lax.axis_index("core") == 0
    for t in range(4):
        a, b = keep[t].reshape(16, 1, 8, 128), got[t].reshape(16, 1, 8, 128)
        even, odd = jnp.where(first, a, b), jnp.where(first, b, a)
        both = jnp.concatenate([even, odd], axis=1).reshape(256, 128).T
        out[:, 2 * t, :] = both[0:64, :]
        out[:, 2 * t + 1, :] = both[64:128, :]


def rows_call(keep, got):
    return pl.pallas_call(
        rows_kernel,
        out_shape=jax.ShapeDtypeStruct((64, 8, 256), jnp.float32),
        in_specs=[VMEM, VMEM],
        out_specs=VMEM,
        compiler_params=pltpu.CompilerParams(vmem_limit_bytes=16 * 2**20),
        cost_estimate=pl.CostEstimate(flops=0, bytes_accessed=2**20, transcendentals=0),
    )(keep, got)


def pin(values):
    return lax.optimization_barrier(values)


def turn(size, shift):
    return [(i, (i + shift) % size) for i in range(size)]


def shards(inverse_root, panel, block_mask, diag_inverse):
    ix, iz, ic = lax.axis_index("x"), lax.axis_index("zh"), lax.axis_index("core")
    col = lax.axis_index("zl") * 4 + lax.axis_index("y")
    swap = [(0, 1), (1, 0)]

    def sum_parts(parts):
        return jnp.sum(parts.astype(jnp.float32), axis=0) * (1.0 / SCALE)

    def send_parts(partial):
        return partial.astype(jnp.float16)

    def around(slab):
        return [lax.ppermute(slab, "x", turn(4, 1)), lax.ppermute(slab, "x", turn(4, -1))]

    def to_columns(value):
        return lax.all_to_all(value, ("zl", "y"), 0, 0, tiled=True)

    def to_rows(value):
        return lax.all_to_all(value, ("x", "zh"), 0, 0, tiled=True)

    other_root = lax.ppermute(inverse_root, "core", swap)
    own = mask_call(block_mask, jnp.transpose(panel, (1, 2, 0)).reshape(64, 2048))
    pieces = pieces_call(own)

    z1, z3 = (lax.ppermute(own, "zh", turn(4, s)) for s in (1, 3))
    near0, pieces = pin((around(own), pieces))
    far0 = lax.ppermute(near0[0], "x", turn(4, 1))
    pieces = to_columns(pieces)
    z1, z3, near0, far0, own, other_root = pin((z1, z3, near0, far0, own, other_root))

    z2 = lax.ppermute(z1, "zh", turn(4, 1))
    near1, near3 = around(z1), around(z3)
    mine = to_rows(hold_call(mark_call(own), pieces.reshape(16, 64, 128)))
    z2, near1, near3 = pin((z2, near1, near3))

    far1, far3 = lax.ppermute(near1[0], "x", turn(4, 1)), lax.ppermute(near3[1], "x", turn(4, -1))
    near2 = around(z2)
    early = send_parts(product_call([own, *near0, far0, z1, *near1, z3], inverse_root, other_root, 58))
    far1, far3, near2, early, mine = pin((far1, far3, near2, early, mine))

    parts = to_columns(early)
    far2 = lax.ppermute(near2[0], "x", turn(4, 1))
    far2 = pin((far2,))[0]

    late = send_parts(product_call([*near3, far1, far3, z2, *near2, far2], inverse_root, other_root, 24))
    late, parts = pin((late, parts))
    other = lax.ppermute(mine, "core", swap)
    keep, give, diag = diag_call(sum_parts(parts), sum_parts(to_columns(late)), mine, other)
    got = lax.ppermute(give, "core", swap)
    here = jnp.sum(to_columns(diag.astype(jnp.float16)).astype(jnp.float32), axis=0)
    panel_inverse = rows_call(keep, got)
    here, panel_inverse = lax.optimization_barrier((here, panel_inverse))
    across = here.reshape(128, 256).T.reshape(2, 16, 8, 128)
    across = jnp.transpose(across, (1, 0, 2, 3))
    here = jnp.sum(to_rows(across), axis=0)
    came = lax.ppermute(here[1], "core", swap)
    even, odd = jnp.where(ic == 0, here[0], came), jnp.where(ic == 0, came, here[0])
    both = jnp.stack([even.reshape(8, 8, 2, 8), odd.reshape(8, 8, 2, 8)], axis=3)
    block = jnp.transpose(both, (1, 0, 2, 3, 4)).reshape(8, 8, 32)
    return panel_inverse, diag_inverse + block


def solution(mesh):
    wide = Mesh(mesh.devices.reshape(4, 4, 2, 2, 4), ("x", "zh", "core", "zl", "y"))
    prow, pcol = ("x", "zh", "core"), ("zl", "y")
    in_specs = (P(prow, pcol), P(pcol, None, prow), P(), P(None, prow, pcol))
    out_specs = (P(prow + pcol, None, None), P(None, prow, pcol))
    return jax.shard_map(shards, mesh=wide, in_specs=in_specs, out_specs=out_specs, check_vma=False)
```

```python
import functools

import jax
import jax.numpy as jnp
from jax import lax
from jax.experimental import pallas as pl
from jax.experimental.pallas import tpu as pltpu
from jax.sharding import Mesh, PartitionSpec as P

EARLY = ((0, 0), (3, 0), (1, 0), (2, 0), (0, 1), (3, 1), (1, 1), (0, 3))
LATE = ((3, 3), (1, 3), (2, 1), (2, 3), (0, 2), (3, 2), (1, 2), (2, 2))
SCALE = 64.0
NT = (((1,), (1,)), ((), ()))
VMEM = pl.BlockSpec(memory_space=pltpu.VMEM)
ANY = pl.BlockSpec(memory_space=pl.ANY)
SMEM = pl.BlockSpec(memory_space=pltpu.SMEM)


def mask_kernel(mask, panel, own):
    col = lax.axis_index("zl") * 4 + lax.axis_index("y")
    upper = lax.broadcasted_iota(jnp.int32, (16, 256), 0) < 8
    for t in range(4):
        rows = slice(16 * t, 16 * t + 16)
        for i in range(8):
            lanes = slice(256 * i, 256 * i + 256)
            here = jnp.where(upper, mask[2 * t, col * 8 + i], mask[2 * t + 1, col * 8 + i]).astype(jnp.float32)
            own[rows, lanes] = (panel[rows, lanes].astype(jnp.float32) * here).astype(own.dtype)


def mask_call(mask, panel):
    return pl.pallas_call(
        mask_kernel,
        out_shape=jax.ShapeDtypeStruct((64, 2048), jnp.bfloat16),
        in_specs=[SMEM, VMEM],
        out_specs=VMEM,
        cost_estimate=pl.CostEstimate(flops=1, bytes_accessed=2**19, transcendentals=0),
    )(mask, panel)


def pieces_kernel(own, pieces):
    ic = lax.axis_index("core")
    low = lax.broadcasted_iota(jnp.int32, (64, 128), 1) < 64
    for b in range(2):
        for u in range(4):
            lanes = [slice(1024 * b + 512 * c + 128 * u, 1024 * b + 512 * c + 128 * u + 128) for c in range(2)]
            even, odd = own[:, lanes[0]].astype(jnp.float32), own[:, lanes[1]].astype(jnp.float32)
            p, q = jnp.where(ic == 0, even, odd), jnp.where(ic == 0, odd, even)
            pieces[2 * u, b] = jnp.where(low, p, pltpu.roll(q, 64, 1)).astype(pieces.dtype)
            pieces[2 * u + 1, b] = jnp.where(low, pltpu.roll(p, 64, 1), q).astype(pieces.dtype)


def pieces_call(own):
    return pl.pallas_call(
        pieces_kernel,
        out_shape=jax.ShapeDtypeStruct((8, 2, 64, 128), jnp.bfloat16),
        in_specs=[VMEM],
        out_specs=VMEM,
        cost_estimate=pl.CostEstimate(flops=1, bytes_accessed=2**19, transcendentals=0),
    )(own)


def product_kernel(*refs):
    slabs, (root, other_root, out, gathered, pair) = refs[:-5], refs[-5:]

    @pl.when(pl.program_id(0) == 0)
    def _():
        start = 0
        for slab in slabs:
            gathered[start:start + slab.shape[0], :] = slab[...]
            start += slab.shape[0]

    for j in range(2):
        pair[128 * j:128 * j + 64, :] = root[64 * j:64 * j + 64, :]
        pair[128 * j + 64:128 * j + 128, :] = other_root[64 * j:64 * j + 64, :]
    prod = lax.dot_general(gathered[...], pair[...], NT, preferred_element_type=jnp.float32)
    out[0] = prod[:, 0:128] * SCALE
    out[1] = prod[:, 128:256] * SCALE


def product_call(slabs, root, other_root, vmem):
    n = sum(slab.shape[0] for slab in slabs)
    return pl.pallas_call(
        product_kernel,
        grid=(4,),
        out_shape=jax.ShapeDtypeStruct((8, n, 128), jnp.float32),
        in_specs=[pl.BlockSpec(slab.shape, lambda t: (0, 0)) for slab in slabs]
        + [pl.BlockSpec((128, 2048), lambda t: (t, 0))] * 2,
        out_specs=pl.BlockSpec((2, n, 128), lambda t: (t, 0, 0)),
        scratch_shapes=[pltpu.VMEM((n, 2048), jnp.bfloat16), pltpu.VMEM((256, 2048), jnp.bfloat16)],
        compiler_params=pltpu.CompilerParams(vmem_limit_bytes=vmem * 2**20),
        cost_estimate=pl.CostEstimate(flops=2 * n * 2048 * 1024, bytes_accessed=2 * n * 2048 + 6 * 2**20, transcendentals=0),
    )(*slabs, root, other_root)


def mark_kernel(source, out):
    out[...] = jnp.zeros_like(out)


def mark_call(value):
    return pl.pallas_call(
        mark_kernel,
        out_shape=jax.ShapeDtypeStruct((8, 128), jnp.float32),
        in_specs=[ANY],
        out_specs=VMEM,
        cost_estimate=pl.CostEstimate(flops=2**34, bytes_accessed=2**12, transcendentals=0),
    )(value)


def hold_kernel(after, source, out):
    pass


def hold_call(after, value):
    return pl.pallas_call(
        hold_kernel,
        out_shape=jax.ShapeDtypeStruct(value.shape, value.dtype),
        in_specs=[ANY, ANY],
        out_specs=ANY,
        input_output_aliases={1: 0},
        cost_estimate=pl.CostEstimate(flops=2**34, bytes_accessed=2**12, transcendentals=0),
    )(after, value)


def diag_kernel(early, late, mine, other, keep, give, diag):
    ix, iz = lax.axis_index("x"), lax.axis_index("zh")
    low = lax.broadcasted_iota(jnp.int32, (8, 128), 1) < 64
    left = mine[...].astype(jnp.float32).reshape(16, 8, 8, 128)
    right = pltpu.roll(other[...].astype(jnp.float32), 64, 2).reshape(16, 8, 8, 128)
    totals, places = [], []
    slabs = [early[64 * i:64 * i + 64, :] for i in range(len(EARLY))] + [late[64 * i:64 * i + 64, :] for i in range(len(LATE))]
    for slab, (dx, dz) in zip(slabs, EARLY + LATE):
        total = slab.reshape(8, 8, 128)
        x, z = lax.rem(ix + dx, 4), lax.rem(iz + 4 - dz, 4)
        totals.append(total)
        places.append((2 * x + lax.div(z, 2), lax.rem(z, 2)))
        for t in range(4):
            even, odd = total[2 * t], total[2 * t + 1]
            keep[t, x, z] = -jnp.where(low, even, pltpu.roll(odd, 64, 1))
            give[t, x, z] = -jnp.where(low, pltpu.roll(even, 64, 1), odd)
    for k in range(8):
        p = jnp.concatenate([total[k] for total in totals], axis=0)
        hi = p.astype(jnp.bfloat16)
        rest = p - hi.astype(jnp.float32)
        mid = rest.astype(jnp.bfloat16)
        lo = (rest - mid.astype(jnp.float32)).astype(jnp.bfloat16)
        m = jnp.concatenate([left[:, k].reshape(128, 128), right[:, k].reshape(128, 128)], axis=0).astype(jnp.bfloat16)
        d = lax.dot_general(lo, m, NT, preferred_element_type=jnp.float32)
        d += lax.dot_general(mid, m, NT, preferred_element_type=jnp.float32)
        d += lax.dot_general(hi, m, NT, preferred_element_type=jnp.float32)
        for i, (column, z) in enumerate(places):
            diag[column, k, z] = d[i * 8:(i + 1) * 8, :]


def diag_call(early, late, mine, other):
    return pl.pallas_call(
        diag_kernel,
        out_shape=(
            jax.ShapeDtypeStruct((4, 4, 4, 8, 128), jnp.float32),
            jax.ShapeDtypeStruct((4, 4, 4, 8, 128), jnp.float32),
            jax.ShapeDtypeStruct((8, 8, 2, 8, 256), jnp.float32),
        ),
        in_specs=[VMEM] * 4,
        out_specs=(VMEM,) * 3,
        compiler_params=pltpu.CompilerParams(vmem_limit_bytes=16 * 2**20),
        cost_estimate=pl.CostEstimate(flops=2 * 8 * 3 * 128 * 128 * 256, bytes_accessed=2**23, transcendentals=0),
    )(early, late, mine, other)


def rows_kernel(keep, got, out):
    first = lax.axis_index("core") == 0
    for t in range(4):
        a, b = keep[t].reshape(16, 1, 8, 128), got[t].reshape(16, 1, 8, 128)
        even, odd = jnp.where(first, a, b), jnp.where(first, b, a)
        both = jnp.concatenate([even, odd], axis=1).reshape(256, 128).T
        out[:, 2 * t, :] = both[0:64, :]
        out[:, 2 * t + 1, :] = both[64:128, :]


def rows_call(keep, got):
    return pl.pallas_call(
        rows_kernel,
        out_shape=jax.ShapeDtypeStruct((64, 8, 256), jnp.float32),
        in_specs=[VMEM, VMEM],
        out_specs=VMEM,
        compiler_params=pltpu.CompilerParams(vmem_limit_bytes=16 * 2**20),
        cost_estimate=pl.CostEstimate(flops=0, bytes_accessed=2**20, transcendentals=0),
    )(keep, got)


def pin(values):
    return lax.optimization_barrier(values)


def turn(size, shift):
    return [(i, (i + shift) % size) for i in range(size)]


def shards(inverse_root, panel, block_mask, diag_inverse):
    ix, iz, ic = lax.axis_index("x"), lax.axis_index("zh"), lax.axis_index("core")
    col = lax.axis_index("zl") * 4 + lax.axis_index("y")
    swap = [(0, 1), (1, 0)]

    def sum_parts(parts):
        return jnp.sum(parts.astype(jnp.float32), axis=0) * (1.0 / SCALE)

    def send_parts(partial):
        return partial.astype(jnp.float16)

    def around(slab):
        return [lax.ppermute(slab, "x", turn(4, 1)), lax.ppermute(slab, "x", turn(4, -1))]

    def to_columns(value):
        return lax.all_to_all(value, ("zl", "y"), 0, 0, tiled=True)

    def to_rows(value):
        return lax.all_to_all(value, ("x", "zh"), 0, 0, tiled=True)

    other_root = lax.ppermute(inverse_root, "core", swap)
    own = mask_call(block_mask, jnp.transpose(panel, (1, 2, 0)).reshape(64, 2048))
    pieces = pieces_call(own)

    z1, z3 = (lax.ppermute(own, "zh", turn(4, s)) for s in (1, 3))
    near0, pieces = pin((around(own), pieces))
    far0 = lax.ppermute(near0[0], "x", turn(4, 1))
    pieces = to_columns(pieces)
    z1, z3, near0, far0, own, other_root = pin((z1, z3, near0, far0, own, other_root))

    z2 = lax.ppermute(z1, "zh", turn(4, 1))
    near1, near3 = around(z1), around(z3)
    mine = to_rows(hold_call(mark_call(own), pieces.reshape(16, 64, 128)))
    z2, near1, near3 = pin((z2, near1, near3))

    far1, far3 = lax.ppermute(near1[0], "x", turn(4, 1)), lax.ppermute(near3[1], "x", turn(4, -1))
    near2 = around(z2)
    early = send_parts(product_call([own, *near0, far0, z1, *near1, z3], inverse_root, other_root, 58))
    near2, early, mine = pin((near2, early, mine))

    parts = to_columns(early)
    far2 = lax.ppermute(near2[0], "x", turn(4, 1))
    far2 = pin((far2,))[0]

    late = send_parts(product_call([*near3, far1, far3, z2, *near2, far2], inverse_root, other_root, 24))
    late, parts = pin((late, parts))
    other = lax.ppermute(mine, "core", swap)
    keep, give, diag = diag_call(sum_parts(parts), sum_parts(to_columns(late)), mine, other)
    got = lax.ppermute(give, "core", swap)
    here = jnp.sum(to_columns(diag.astype(jnp.float16)).astype(jnp.float32), axis=0)
    panel_inverse = rows_call(keep, got)
    here, panel_inverse = lax.optimization_barrier((here, panel_inverse))
    across = here.reshape(128, 256).T.reshape(2, 16, 8, 128)
    across = jnp.transpose(across, (1, 0, 2, 3))
    here = jnp.sum(to_rows(across), axis=0)
    came = lax.ppermute(here[1], "core", swap)
    even, odd = jnp.where(ic == 0, here[0], came), jnp.where(ic == 0, came, here[0])
    both = jnp.stack([even.reshape(8, 8, 2, 8), odd.reshape(8, 8, 2, 8)], axis=3)
    block = jnp.transpose(both, (1, 0, 2, 3, 4)).reshape(8, 8, 32)
    return panel_inverse, diag_inverse + block


def solution(mesh):
    wide = Mesh(mesh.devices.reshape(4, 4, 2, 2, 4), ("x", "zh", "core", "zl", "y"))
    prow, pcol = ("x", "zh", "core"), ("zl", "y")
    in_specs = (P(prow, pcol), P(pcol, None, prow), P(), P(None, prow, pcol))
    out_specs = (P(prow + pcol, None, None), P(None, prow, pcol))
    return jax.shard_map(shards, mesh=wide, in_specs=in_specs, out_specs=out_specs, check_vma=False)
```
